256 devices in a mesh: seq: 32 (over z, x), head: 8 (over y, core).
Axes of the slice: x: 4, y: 4, z: 8, core: 2. Of those that a mesh axis runs over, the one named last changes fastest.
Arguments:
- query: bfloat16 [16384, 16, 128], P('seq', 'head'), may hold values from -60 to 60
- key: bfloat16 [16384, 16, 128], P('seq', 'head'), may hold values from -6 to 6
- value: bfloat16 [16384, 16, 128], P('seq', 'head'), may hold values from -6 to 6
- reflect: bfloat16 [16384, 16, 128], P('seq', 'head'), may hold values from -8 to 8
- block_mask: int32 [16, 128, 128], P('head'), may hold values from 0 to 1, as said below
- out_weight: bfloat16 [2048, 2048], P('head'), may hold values from -0.125 to 0.125
Outputs:
- mixed: bfloat16 [16384, 2048], P('seq', 'head')
The draws below stay inside these ranges and needn't reach their ends.
Inputs may be any that keep to these rules, and one draw needn't show every extreme that they name: block_mask[h, b, b] = 1 for every head h and block b.
All inputs are finite; a program needn't handle non-finite values.
Results may differ from the reference program's by a relative error of at most 0.011.
The reference program's roundings to bfloat16 on the way count: a program that leaves them out, or rounds other values in their place, can miss the bound.
Values may be sent and summed in bfloat16 or wider, within the bound.
No kernel may reach another device: no remote copies, remote signals or barrier semaphores. Data moves between devices by JAX's collectives and lax.ppermute only.
A program may use at most 64 MiB of HBM per device.

```python
import jax
import jax.numpy as jnp
from jax import lax

HEADS = 16
DH = 128
D = 2048
BLK = 128
L_DEV = 512
SEQ = 16384
NBLK = 128


def draw_query(key, part):
    key = jax.random.fold_in(key, 11)
    first_key = jax.random.fold_in(key, 0)
    base_values = jax.random.truncated_normal(first_key, -4.0, 4.0, (SEQ, HEADS, DH), jnp.float32)
    return (1.6 * base_values).astype(jnp.bfloat16)


def draw_reflect(key, part):
    key = jax.random.fold_in(key, 37)
    first_key = jax.random.fold_in(key, 0)
    base_values = jax.random.truncated_normal(first_key, -6.0, 6.0, (SEQ, HEADS, DH), jnp.float32)
    return base_values.astype(jnp.bfloat16)


def draw_block_mask(key, part):
    key = jax.random.fold_in(key, 23)
    first_key, second_key = jax.random.split(key)
    levels = jax.random.randint(first_key, (HEADS, 1, 1), 1, 10)
    rolls = jax.random.randint(second_key, (HEADS, NBLK, NBLK), 0, 10)
    picked = (rolls < levels).astype(jnp.int32)
    diagonal = jnp.eye(NBLK, dtype=jnp.int32)[None, :, :]
    return jnp.maximum(picked, diagonal)


def level_of(own_key, dims, shards, least, high):
    gain = 1.0
    for position, parts in shards:
        heights = jax.random.uniform(jax.random.fold_in(jax.random.fold_in(own_key, 6), position), (parts,), jnp.float32, least / len(shards), high / len(shards))
        gain = gain * jnp.repeat(jnp.exp(heights), dims[position] // parts).reshape((-1,) + (1,) * (len(dims) - 1 - position))
    return gain


def normal_values(own_key, shape, scale, reach, cuts=(), kind=jnp.bfloat16):
    array = scale * jax.random.normal(own_key, shape, jnp.float32)
    if cuts:
        array = array * level_of(own_key, shape, cuts, -0.22, 0.18)
    return jnp.clip(array, -reach, reach).astype(kind)


def setup_inputs(seed: int = 0) -> dict:
    arg_keys = jax.random.split(jax.random.key(seed), 7)
    query = draw_query(jax.random.fold_in(arg_keys[6], 71), 0)
    key = normal_values(arg_keys[1], (SEQ, HEADS, DH), 1.6, 6.0, ((0, 32), (1, 8)))
    value = normal_values(arg_keys[2], (SEQ, HEADS, DH), 1.0, 6.0, ((0, 32), (1, 8)))
    reflect = draw_reflect(jax.random.fold_in(arg_keys[6], 71), 0)
    block_mask = draw_block_mask(jax.random.fold_in(arg_keys[6], 71), 0)
    out_weight = normal_values(arg_keys[5], (HEADS * DH, D), (HEADS * DH) ** -0.5, 0.125, ((0, 8),))
    return {"query": query, "key": key, "value": value, "reflect": reflect, "block_mask": block_mask, "out_weight": out_weight}


HIGH = lax.Precision.HIGHEST
EPSILON = 1e-06
FLOOR_SCORE = -1e+30

def normalize_rows(values):
    values = values.astype(jnp.float32)
    return values * lax.rsqrt(lax.optimization_barrier(jnp.sum(values * values, axis=-1, keepdims=True)) + EPSILON)

def upper_inverse(strict_upper):
    block_size = strict_upper.shape[-1]
    identity = jnp.eye(block_size, dtype=jnp.float32)
    power = -2.0 * strict_upper
    result = identity + power
    steps = block_size.bit_length() - 1
    for step in range(steps - 1):
        power = jnp.einsum('...ab,...bc->...ac', power, power, precision=HIGH)
        result = jnp.einsum('...ab,...bc->...ac', result, identity + power, precision=HIGH)
    return 2.0 * result

def block_factors(unit_dirs):
    feature_width = unit_dirs.shape[-1]
    intersections = jnp.einsum('...ad,...bd->...ab', unit_dirs, unit_dirs, precision=HIGH)
    triangle = upper_inverse(jnp.triu(intersections, 1))
    spread = jnp.einsum('...ab,...be->...ae', triangle, unit_dirs, precision=HIGH)
    block_whole = jnp.eye(feature_width, dtype=jnp.float32) - jnp.einsum('...ad,...ae->...de', unit_dirs, spread, precision=HIGH)
    return (triangle, block_whole)

def apply_local(row_data, unit_dirs, triangle):
    block_size = row_data.shape[-2]
    projected = jnp.einsum('...md,...kd->...mk', row_data, unit_dirs, precision=HIGH)
    lower_mask = jnp.tril(jnp.ones((block_size, block_size), jnp.float32))
    coefficients = jnp.einsum('...mk,...rk->...mr', projected * lower_mask, triangle, precision=HIGH)
    return row_data - jnp.einsum('...mr,...rd->...md', coefficients, unit_dirs, precision=HIGH)

def reference(query, key, value, reflect, block_mask, out_weight):
    features = query.shape[2]
    count = SEQ // BLK
    identity = jnp.eye(features, dtype=jnp.float32)
    scale = features ** (-0.5)

    def rotate_head(head_query, head_key, head_reflect):
        unit_dirs = normalize_rows(head_reflect).reshape(count, BLK, features)
        triangle, block_whole = block_factors(unit_dirs)
        local_query = apply_local(head_query.astype(jnp.float32).reshape(count, BLK, features), unit_dirs, triangle)
        local_key = apply_local(head_key.astype(jnp.float32).reshape(count, BLK, features), unit_dirs, triangle)

        def advance(frame, items):
            part_query, part_key, blockmat = items
            turned_query = jnp.einsum('md,ed->me', part_query, frame, precision=HIGH)
            turned_key = jnp.einsum('md,ed->me', part_key, frame, precision=HIGH)
            return (jnp.dot(frame, blockmat, precision=HIGH), (turned_query, turned_key))
        final_frame, outputs = lax.scan(advance, identity, (local_query, local_key, block_whole))
        turned_query = outputs[0].reshape(SEQ, features).astype(jnp.bfloat16)
        turned_key = outputs[1].reshape(SEQ, features).astype(jnp.bfloat16)
        return (turned_query, turned_key)

    def attend_head(items):
        head_query, head_key, head_value, head_reflect, head_mask = items
        turned_query, turned_key = rotate_head(head_query, head_key, head_reflect)
        turned_query = lax.optimization_barrier(turned_query).astype(jnp.float32)
        key_float = lax.optimization_barrier(turned_key).astype(jnp.float32)
        value_float = head_value.astype(jnp.float32)
        key_pos = lax.iota(jnp.int32, SEQ)

        def one_block(block_index):
            start = (block_index * L_DEV).astype(jnp.int32)
            queries = lax.dynamic_slice_in_dim(turned_query, start, L_DEV, 0)
            scores = jnp.einsum('qd,kd->qk', queries, key_float, precision=HIGH) * scale
            query_pos = start + lax.iota(jnp.int32, L_DEV)
            mask_rows = lax.dynamic_slice_in_dim(head_mask, (start // BLK).astype(jnp.int32), L_DEV // BLK, 0)
            block_full = jnp.broadcast_to(mask_rows[:, None, :, None] == 1, (L_DEV // BLK, BLK, count, BLK)).reshape(L_DEV, SEQ)
            allowed = block_full & (key_pos[None, :] <= query_pos[:, None])
            row_max = lax.optimization_barrier(jnp.max(jnp.where(allowed, scores, FLOOR_SCORE), axis=-1, keepdims=True))
            raw_weights = jnp.where(allowed, jnp.exp(scores - row_max), 0.0)
            totals = lax.optimization_barrier(jnp.sum(raw_weights, axis=-1, keepdims=True))
            rounded = lax.optimization_barrier(raw_weights.astype(jnp.bfloat16)).astype(jnp.float32)
            summed = jnp.einsum('qk,kd->qd', rounded, value_float, precision=HIGH)
            return (summed / totals).astype(jnp.bfloat16)
        pieces = lax.map(one_block, jnp.arange(SEQ // L_DEV, dtype=jnp.int32))
        return pieces.reshape(SEQ, features)
    attended = lax.map(attend_head, (query.transpose(1, 0, 2), key.transpose(1, 0, 2), value.transpose(1, 0, 2), reflect.transpose(1, 0, 2), block_mask))
    attended = lax.optimization_barrier(attended).astype(jnp.float32)
    weight_heads = out_weight.astype(jnp.float32).reshape(HEADS, features, out_weight.shape[1])
    mixed = jnp.einsum('hsd,hde->se', attended, weight_heads, precision=HIGH)
    return mixed.astype(jnp.bfloat16)
```

```python
from functools import partial
import math

import jax
import jax.numpy as jnp
from jax import lax
from jax.experimental import pallas as pl
from jax.experimental.pallas import tpu as pltpu
from jax.sharding import PartitionSpec as P

BLK = 128
DH = 128
XN = 4
ZN = 8
HL = 2
NB = 4
EPSILON = 1e-06
LOW = -1e30
SCALE = math.log2(math.e) / math.sqrt(DH)
f32 = jnp.float32
bf16 = jnp.bfloat16
NN = ((1,), (0,))
NT = ((1,), (1,))
TN = ((0,), (0,))
VMEM = pl.BlockSpec(memory_space=pltpu.VMEM)
SMEM = pl.BlockSpec(memory_space=pltpu.SMEM)


def params():
    return pltpu.CompilerParams(vmem_limit_bytes=48 * 1024 * 1024)


def dot1(a, b, dims=NN):
    return lax.dot_general(a, b, (dims, ((), ())), preferred_element_type=f32)


def halves(a):
    high = a.astype(bf16)
    return high, (a - high.astype(f32)).astype(bf16)


def dot3(a, b, dims=NN):
    ah, al = halves(a)
    bh, bl = halves(b)
    return dot1(ah, bh, dims) + (dot1(al, bh, dims) + dot1(ah, bl, dims))


def eye():
    row = lax.broadcasted_iota(jnp.int32, (BLK, BLK), 0)
    col = lax.broadcasted_iota(jnp.int32, (BLK, BLK), 1)
    return jnp.where(row == col, 1.0, 0.0).astype(f32)


def unit_rows(values):
    values = values.astype(f32)
    return values * lax.rsqrt(jnp.sum(values * values, axis=-1, keepdims=True) + EPSILON)


def factor_kernel(reflect_ref, tri_ref, frames_ref, total_ref):
    row = lax.broadcasted_iota(jnp.int32, (BLK, BLK), 0)
    col = lax.broadcasted_iota(jnp.int32, (BLK, BLK), 1)
    ident = jnp.where(row == col, 1.0, 0.0).astype(f32)
    items = [(h, b) for h in range(HL) for b in range(NB)]
    units = [unit_rows(reflect_ref[h, pl.ds(b * BLK, BLK), :]) for h, b in items]
    grams = [2.0 * dot3(u, u, NT) for u in units]
    inv = [ident - jnp.where((row // 2 == col // 2) & (row < col), g, 0.0) for g in grams]
    size = 2
    while size < BLK:
        off = (row // (2 * size) == col // (2 * size)) & (row // size < col // size)
        mids = [dot3(x, jnp.where(off, g, 0.0)) for x, g in zip(inv, grams)]
        inv = [x - dot3(m, x) for x, m in zip(inv, mids)]
        size *= 2
    wholes = []
    for (h, b), u, x in zip(items, units, inv):
        tri = 2.0 * x
        tri_ref[h, b] = tri
        wholes.append(ident - dot3(u, dot3(tri, u), TN))
    frames = [wholes[h * NB] for h in range(HL)]
    for b in range(1, NB):
        for h in range(HL):
            frames_ref[h, b - 1] = frames[h]
        frames = [dot3(frames[h], wholes[h * NB + b]) for h in range(HL)]
    for h in range(HL):
        total_ref[h] = frames[h]


def local_kernel(query_ref, key_ref, reflect_ref, tri_ref, frames_ref, qt_ref, k_ref):
    row = lax.broadcasted_iota(jnp.int32, (2 * BLK, BLK), 0) % BLK
    col = lax.broadcasted_iota(jnp.int32, (2 * BLK, BLK), 1)
    lower = col <= row
    for h in range(HL):
        for b in range(NB):
            here = pl.ds(b * BLK, BLK)
            unit = unit_rows(reflect_ref[h, here, :])
            uh, ul = halves(unit)
            both = jnp.concatenate([query_ref[h, here, :], key_ref[h, here, :]], axis=0)
            proj = dot1(both, uh, NT) + dot1(both, ul, NT)
            coef = dot3(jnp.where(lower, proj, 0.0), tri_ref[h, b], NT)
            turned = both.astype(f32) - dot3(coef, unit)
            if b > 0:
                turned = dot3(turned, frames_ref[h, b - 1], NT)
            qt_ref[h, b] = turned[:BLK].T
            k_ref[h, b] = turned[BLK:]


def row_kernel(where_ref, own_ref, one_ref, two_ref, three_ref, before_ref, total_ref):
    x = where_ref[1]
    for h in range(HL):
        cands = [own_ref[h], one_ref[h], two_ref[h], three_ref[h]]

        def pick(i):
            out = cands[0]
            for k in range(1, XN):
                out = jnp.where((x - k) % XN == i, cands[k], out)
            return out

        first = pick(0)
        second = dot3(first, pick(1))
        third = dot3(second, pick(2))
        before = jnp.where(x == 0, eye(), first)
        before = jnp.where(x == 2, second, before)
        before_ref[h] = jnp.where(x == 3, third, before)
        total_ref[h] = dot3(third, pick(3))


def hop_kernel(step, where_ref, left_ref, total_ref, before_ref, total_out, before_out):
    z = where_ref[0]
    for h in range(HL):
        left = jnp.where(z >= step, left_ref[h], eye())
        total_out[h] = dot3(left, total_ref[h])
        before_out[h] = dot3(left, before_ref[h])


def turn_kernel(where_ref, left_ref, before_ref, qt_ref, k_ref, qt_out, k_out):
    z = where_ref[0]
    for h in range(HL):
        left = jnp.where(z >= 4, left_ref[h], eye())
        frame = dot3(left, before_ref[h])
        for b in range(NB):
            qt_out[h, b] = dot3(frame, qt_ref[h, b]).astype(bf16)
            k_out[h, b] = dot3(k_ref[h, b], frame, NT).astype(bf16)


def attend_kernel(where_ref, count_ref, list_ref, *refs):
    queries = refs[:XN]
    keys = refs[XN : XN + ZN]
    values_ref = refs[XN + ZN]
    out_ref, lse_ref = refs[XN + ZN + 1 : XN + ZN + 3]
    scratch = refs[XN + ZN + 3 :]
    k_s, bias_s = scratch[0], scratch[1]
    q_s = scratch[2 : 2 + XN]
    m_s = scratch[2 + XN : 2 + 2 * XN]
    l_s = scratch[2 + 2 * XN : 2 + 3 * XN]
    acc_s = scratch[2 + 3 * XN : 2 + 4 * XN]
    z = where_ref[0]
    for j in range(ZN):
        source = (z - j + ZN) % ZN
        k_s[source] = keys[j][...]
    krow = lax.broadcasted_iota(jnp.int32, (BLK, BLK), 0)
    qcol = lax.broadcasted_iota(jnp.int32, (BLK, BLK), 1)
    bias_s[0] = jnp.zeros((BLK, BLK), f32)
    bias_s[1] = jnp.where(krow <= qcol, 0.0, LOW).astype(f32)
    bias_s[2] = jnp.full((BLK, BLK), LOW, f32)
    for a in range(XN):
        for h in range(HL):
            for i in range(NB):
                q_s[a][h * NB + i] = queries[a][h, i]
        q_s[a][HL * NB] = jnp.zeros((DH, BLK), bf16)
        m_s[a][...] = jnp.full(m_s[a].shape, LOW, f32)
        l_s[a][...] = jnp.zeros(l_s[a].shape, f32)
        acc_s[a][...] = jnp.zeros(acc_s[a].shape, f32)

    def step(t, carry):
        for a in range(XN):
            code = list_ref[a, t]
            qi = code & 15
            h = (code >> 2) & 1
            z1, j1 = (code >> 6) & 7, (code >> 4) & 3
            z2, j2 = (code >> 11) & 7, (code >> 9) & 3
            b1 = (code >> 14) & 3
            b2 = (code >> 16) & 3
            qt = q_s[a][qi]
            s1 = dot1(k_s[z1, h, j1], qt) + bias_s[b1]
            s2 = dot1(k_s[z2, h, j2], qt) + bias_s[b2]
            top = jnp.max(jnp.maximum(s1, s2), axis=0, keepdims=True) * SCALE
            m_old = m_s[a][qi]
            m_new = jnp.maximum(m_old, top)
            alpha = jnp.exp2(m_old - m_new)
            m_row = m_new[:1]
            p1 = jnp.exp2(s1 * SCALE - m_row)
            p2 = jnp.exp2(s2 * SCALE - m_row)
            l_s[a][qi] = l_s[a][qi] * alpha + jnp.sum(p1 + p2, axis=0, keepdims=True)
            m_s[a][qi] = m_new
            pt = jnp.concatenate([p1.astype(bf16), p2.astype(bf16)], axis=0)
            vt = jnp.concatenate([values_ref[z1, h, j1], values_ref[z2, h, j2]], axis=1)
            acc_s[a][qi] = acc_s[a][qi] * alpha[:1] + dot1(vt, pt)
        return carry

    most = count_ref[0]
    for a in range(1, XN):
        most = jnp.maximum(most, count_ref[a])
    lax.fori_loop(0, most, step, 0)
    for a in range(XN):
        for n in range(HL * NB):
            total = l_s[a][n][:1]
            some = total > 0.0
            safe = jnp.where(some, total, 1.0)
            out_ref[a, n] = (acc_s[a][n] * (1.0 / safe)).astype(bf16)
            lse_ref[a, pl.ds(n, 1), :] = jnp.where(some, m_s[a][n][:1] + jnp.log2(safe), LOW)


def project_kernel(*refs):
    parts = refs[:XN]
    lses = refs[XN : 2 * XN]
    weight_ref = refs[2 * XN]
    out_ref = refs[2 * XN + 1]
    for i in range(NB):
        mixed = []
        for h in range(HL):
            n = h * NB + i
            rows = [lse[pl.ds(n, 1), :] for lse in lses]
            top = jnp.maximum(jnp.maximum(rows[0], rows[1]), jnp.maximum(rows[2], rows[3]))
            shares = [jnp.exp2(r - top) for r in rows]
            scale = 1.0 / (shares[0] + shares[1] + shares[2] + shares[3])
            acc = parts[0][n].astype(f32) * (shares[0] * scale)
            for part, share in zip(parts[1:], shares[1:]):
                acc = acc + part[n].astype(f32) * (share * scale)
            mixed.append(acc.astype(bf16))
        rows = jnp.concatenate(mixed, axis=0).T
        for c in range(0, weight_ref.shape[1], 512):
            out_ref[pl.ds(i * BLK, BLK), pl.ds(c, 512)] = dot1(
                rows, weight_ref[:, pl.ds(c, 512)]
            ).astype(bf16)


def call(kernel, outs, ins, scratch=(), smem=0, flops=1e9):
    size = sum(math.prod(a.shape) * a.dtype.itemsize for a in ins)
    return pl.pallas_call(
        kernel,
        out_shape=outs,
        in_specs=[SMEM] * smem + [VMEM] * (len(ins) - smem),
        out_specs=jax.tree.map(lambda _: VMEM, outs),
        scratch_shapes=list(scratch),
        compiler_params=params(),
        cost_estimate=pl.CostEstimate(flops=int(flops), bytes_accessed=size, transcendentals=0),
    )(*ins)


def shape(*dims, dtype=f32):
    return jax.ShapeDtypeStruct(dims, dtype)


def work_lists(block_mask, z, x):
    heads = lax.broadcasted_iota(jnp.int32, (HL, XN, NB, ZN * NB), 1)
    lane_x = (x - heads + XN) % XN
    qpos = (z * XN + lane_x) * NB + lax.broadcasted_iota(jnp.int32, heads.shape, 2)
    kk = lax.broadcasted_iota(jnp.int32, heads.shape, 3)
    kpos = ((kk // NB) * XN + x) * NB + kk % NB
    rows = lax.dynamic_slice_in_dim(block_mask, z * XN * NB, XN * NB, 1)
    rows = rows.reshape(HL, XN, NB, ZN, XN, NB)
    rows = lax.dynamic_index_in_dim(rows, x, 4, keepdims=False).reshape(HL, XN, NB, ZN * NB)
    lanes = jnp.stack(
        [lax.dynamic_index_in_dim(rows, (x - a + XN) % XN, 1, keepdims=False) for a in range(XN)], 1
    )
    allowed = (lanes == 1) & (kpos <= qpos)
    flag = allowed.astype(jnp.int32)
    entry = kk + ZN * NB * jnp.where(kpos == qpos, 1, 0)
    before = jnp.sum(
        jnp.where(jnp.arange(ZN * NB)[:, None] < jnp.arange(ZN * NB)[None, :], flag[..., :, None], 0), -2
    )
    slot = jnp.where(allowed, before, -1)
    hit = slot[..., :, None] == jnp.arange(ZN * NB)[None, :]
    found = jnp.sum(hit.astype(jnp.int32), -2)
    ordered = jnp.sum(jnp.where(hit, entry[..., :, None], 0), -2)
    ordered = jnp.where(found > 0, ordered, 2 * ZN * NB)
    pairs = ordered.reshape(HL, XN, NB, ZN * NB // 2, 2)
    first, second = pairs[..., 0], pairs[..., 1]
    valid = found.reshape(HL, XN, NB, ZN * NB // 2, 2)[..., 0]
    qi = (
        lax.broadcasted_iota(jnp.int32, valid.shape, 0) * NB
        + lax.broadcasted_iota(jnp.int32, valid.shape, 2)
    )
    span = ZN * NB
    code = (
        qi
        + ((first % span) << 4)
        + ((second % span) << 9)
        + ((first // span) << 14)
        + ((second // span) << 16)
    )
    code = code.transpose(1, 0, 2, 3).reshape(XN, -1)
    valid = valid.transpose(1, 0, 2, 3).reshape(XN, -1)
    many = code.shape[1]
    place = jnp.sum(
        jnp.where(jnp.arange(many)[:, None] < jnp.arange(many)[None, :], valid[..., :, None], 0), -2
    )
    place = jnp.where(valid > 0, place, -1)
    put = place[..., :, None] == jnp.arange(many)[None, :]
    filled = jnp.sum(put.astype(jnp.int32), -2)
    lists = jnp.sum(jnp.where(put, code[..., :, None], 0), -2)
    dummy = HL * NB + (2 << 16)
    lists = jnp.where(filled > 0, lists, dummy)
    return jnp.sum(valid, -1), lists


def along_z(value, step):
    pairs = [(z * XN + x, ((z + step) % ZN) * XN + x) for z in range(ZN) for x in range(XN)]
    return lax.ppermute(value, "seq", pairs)


def up_z(value, step):
    pairs = [(z * XN + x, (z + step) * XN + x) for z in range(ZN - step) for x in range(XN)]
    return lax.ppermute(value, "seq", pairs)


def along_x(value, step):
    pairs = [(z * XN + x, z * XN + (x + step) % XN) for z in range(ZN) for x in range(XN)]
    return lax.ppermute(value, "seq", pairs)


def on_device(query, key, value, reflect, block_mask, out_weight):
    here = lax.axis_index("seq")
    z, x = here // XN, here % XN
    where = jnp.stack([z, x]).astype(jnp.int32)
    columns = [[z * XN + x for z in range(ZN)] for x in range(XN)]
    reflect_h = reflect.transpose(1, 0, 2)
    values_t = value.reshape(NB, BLK, HL, DH).transpose(2, 0, 3, 1)
    values_all = lax.all_gather(values_t, "seq", axis=0, axis_index_groups=columns)
    square = shape(HL, DH, DH)
    blocks = shape(HL, NB, BLK, DH)
    tri, frames, total = call(
        factor_kernel, (blocks, shape(HL, NB - 1, DH, DH), square), (reflect_h,), flops=2e9
    )
    others = [along_x(total, k) for k in range(1, XN)]
    q_local, k_local = call(
        local_kernel,
        (blocks, blocks),
        (query.transpose(1, 0, 2), key.transpose(1, 0, 2), reflect_h, tri, frames),
        flops=2e9,
    )
    counts, lists = work_lists(block_mask, z, x)
    before, total = call(row_kernel, (square, square), (where, total, *others), smem=1)
    for step in (1, 2):
        left = up_z(total, step)
        total, before = call(
            partial(hop_kernel, step), (square, square), (where, left, total, before), smem=1
        )
    left = up_z(total, 4)
    q_turned, k_turned = call(
        turn_kernel,
        (shape(HL, NB, DH, BLK, dtype=bf16), shape(HL, NB, BLK, DH, dtype=bf16)),
        (where, left, before, q_local, k_local),
        smem=1,
    )
    lanes = [q_turned] + [along_x(q_turned, k) for k in range(1, XN)]
    rows = [None] * ZN
    rows[0] = k_turned
    for j in range(1, 5):
        rows[j] = along_z(rows[j - 1], 1)
    for j in range(1, 4):
        rows[ZN - j] = along_z(rows[(ZN - j + 1) % ZN], -1)
    state = HL * NB + 1
    parts, lse = call(
        attend_kernel,
        (shape(XN, HL * NB, DH, BLK, dtype=bf16), shape(XN, HL * NB, BLK)),
        (where, counts, lists, *lanes, *rows, values_all),
        scratch=[pltpu.VMEM((ZN, HL, NB, BLK, DH), bf16), pltpu.VMEM((3, BLK, BLK), f32)]
        + [pltpu.VMEM((state, DH, BLK), bf16)] * XN
        + [pltpu.VMEM((state, 8, BLK), f32)] * XN
        + [pltpu.VMEM((state, 8, BLK), f32)] * XN
        + [pltpu.VMEM((state, DH, BLK), f32)] * XN,
        smem=3,
        flops=2e10,
    )
    got = [parts[0]] + [along_x(parts[a], -a) for a in range(1, XN)]
    got_lse = [lse[0]] + [along_x(lse[a], -a) for a in range(1, XN)]
    terms = call(
        project_kernel,
        shape(NB * BLK, out_weight.shape[1], dtype=bf16),
        (*got, *got_lse, out_weight),
    )
    return lax.psum_scatter(terms, "head", scatter_dimension=1, tiled=True)


def solution(mesh):
    in_specs = (
        P("seq", "head", None),
        P("seq", "head", None),
        P("seq", "head", None),
        P("seq", "head", None),
        P("head", None, None),
        P("head", None),
    )
    out_specs = P("seq", "head")
    return jax.shard_map(
        on_device, mesh=mesh, in_specs=in_specs, out_specs=out_specs, check_vma=False
    )
```

```python
from functools import partial
import math

import jax
import jax.numpy as jnp
from jax import lax
from jax.experimental import pallas as pl
from jax.experimental.pallas import tpu as pltpu
from jax.sharding import PartitionSpec as P

BLK = 128
DH = 128
XN = 4
ZN = 8
HL = 2
NB = 4
YN = 4
QB = HL * XN * NB
LANES = 8
LSE = 16
SLOTS = 256
CALLS = ((0,), (1, 7), (2, 6), (3, 5, 4))
EPSILON = 1e-06
LOW = -1e30
SCALE = math.log2(math.e) / math.sqrt(DH)
f32 = jnp.float32
bf16 = jnp.bfloat16
NN = ((1,), (0,))
NT = ((1,), (1,))
TN = ((0,), (0,))
VMEM = pl.BlockSpec(memory_space=pltpu.VMEM)
SMEM = pl.BlockSpec(memory_space=pltpu.SMEM)


def params(mib):
    return pltpu.CompilerParams(vmem_limit_bytes=mib * 1024 * 1024)


def dot1(a, b, dims=NN):
    return lax.dot_general(a, b, (dims, ((), ())), preferred_element_type=f32)


def halves(a):
    high = a.astype(bf16)
    return high, (a - high.astype(f32)).astype(bf16)


def dot3(a, b, dims=NN):
    ah, al = halves(a)
    bh, bl = halves(b)
    return dot1(ah, bh, dims) + (dot1(al, bh, dims) + dot1(ah, bl, dims))


def eye():
    row = lax.broadcasted_iota(jnp.int32, (BLK, BLK), 0)
    col = lax.broadcasted_iota(jnp.int32, (BLK, BLK), 1)
    return jnp.where(row == col, 1.0, 0.0).astype(f32)


def unit_rows(values):
    values = values.astype(f32)
    return values * lax.rsqrt(jnp.sum(values * values, axis=-1, keepdims=True) + EPSILON)


def factor_kernel(reflect_ref, tri_ref, frames_ref, total_ref):
    row = lax.broadcasted_iota(jnp.int32, (BLK, BLK), 0)
    col = lax.broadcasted_iota(jnp.int32, (BLK, BLK), 1)
    ident = jnp.where(row == col, 1.0, 0.0).astype(f32)
    items = [(h, b) for h in range(HL) for b in range(NB)]
    units = [unit_rows(reflect_ref[h, pl.ds(b * BLK, BLK), :]) for h, b in items]
    grams = [2.0 * dot3(u, u, NT) for u in units]
    inv = [ident - jnp.where((row // 2 == col // 2) & (row < col), g, 0.0) for g in grams]
    size = 2
    while size < BLK:
        off = (row // (2 * size) == col // (2 * size)) & (row // size < col // size)
        mids = [dot3(x, jnp.where(off, g, 0.0)) for x, g in zip(inv, grams)]
        inv = [x - dot3(m, x) for x, m in zip(inv, mids)]
        size *= 2
    wholes = []
    for (h, b), u, x in zip(items, units, inv):
        tri = 2.0 * x
        tri_ref[h, b] = tri
        wholes.append(ident - dot3(u, dot3(tri, u), TN))
    frames = [wholes[h * NB] for h in range(HL)]
    for b in range(1, NB):
        for h in range(HL):
            frames_ref[h, b - 1] = frames[h]
        frames = [dot3(frames[h], wholes[h * NB + b]) for h in range(HL)]
    for h in range(HL):
        total_ref[h] = frames[h]


def local_kernel(query_ref, key_ref, reflect_ref, tri_ref, frames_ref, qt_ref, k_ref):
    row = lax.broadcasted_iota(jnp.int32, (2 * BLK, BLK), 0) % BLK
    col = lax.broadcasted_iota(jnp.int32, (2 * BLK, BLK), 1)
    lower = col <= row
    for h in range(HL):
        for b in range(NB):
            here = pl.ds(b * BLK, BLK)
            unit = unit_rows(reflect_ref[h, here, :])
            uh, ul = halves(unit)
            both = jnp.concatenate([query_ref[h, here, :], key_ref[h, here, :]], axis=0)
            proj = dot1(both, uh, NT) + dot1(both, ul, NT)
            coef = dot3(jnp.where(lower, proj, 0.0), tri_ref[h, b], NT)
            turned = both.astype(f32) - dot3(coef, unit)
            if b > 0:
                turned = dot3(turned, frames_ref[h, b - 1], NT)
            qt_ref[h, b] = turned[:BLK].T
            k_ref[h, b] = turned[BLK:]


def row_kernel(where_ref, own_ref, one_ref, two_ref, three_ref, before_ref, total_ref):
    x = where_ref[1]
    for h in range(HL):
        cands = [own_ref[h], one_ref[h], two_ref[h], three_ref[h]]

        def pick(i):
            out = cands[0]
            for k in range(1, XN):
                out = jnp.where((x - k + XN) % XN == i, cands[k], out)
            return out

        first = pick(0)
        second = dot3(first, pick(1))
        third = dot3(second, pick(2))
        for a in range(XN):
            lane = (x - a + XN) % XN
            before = jnp.where(lane == 0, eye(), first)
            before = jnp.where(lane == 2, second, before)
            before_ref[a, h] = jnp.where(lane == 3, third, before)
        total_ref[h] = dot3(third, pick(3))


def hop_kernel(step, where_ref, left_ref, total_ref, *refs):
    z = where_ref[0]
    total_out, chain_out = refs[-2:]
    for h in range(HL):
        left = jnp.where(z >= step, left_ref[h], eye())
        total_out[h] = dot3(left, total_ref[h])
        chain_out[h] = left if step == 1 else dot3(left, refs[0][h])


def turn_key_kernel(where_ref, left_ref, chain_ref, before_ref, k_ref, k_out, chain_out):
    z = where_ref[0]
    for h in range(HL):
        left = jnp.where(z >= 4, left_ref[h], eye())
        chain = dot3(left, chain_ref[h])
        chain_out[h] = chain
        frame = dot3(chain, before_ref[0, h])
        for b in range(NB):
            k_out[h, b] = dot3(k_ref[h, b], frame, NT).astype(bf16)


def turn_query_kernel(chain_ref, before_ref, *refs):
    lanes, out_ref = refs[:XN], refs[XN]
    for a in range(XN):
        for h in range(HL):
            frame = dot3(chain_ref[h], before_ref[a, h])
            for b in range(NB):
                out_ref[(h * XN + a) * NB + b] = dot3(frame, lanes[a][h, b]).astype(bf16)
    out_ref[QB] = jnp.zeros((DH, BLK), bf16)


def attend_kernel(index, first, last, rows, *refs):
    refs = list(refs)
    list_ref, q_ref = refs[:2]
    keys, values = refs[2 : 2 + rows], refs[2 + rows : 2 + 2 * rows]
    refs = refs[2 + 2 * rows :]
    carried = None
    if not first:
        carried, refs = refs[:3], refs[3:]
    if last:
        out_ref, m_s, l_s, acc_s, k_s, v_s, bias_s, p_s, a_s = refs
    else:
        m_s, l_s, acc_s, k_s, v_s, bias_s, p_s, a_s = refs
    for r in range(rows):
        k_s[r] = keys[r][...]
        v_s[r] = values[r][...]
    krow = lax.broadcasted_iota(jnp.int32, (BLK, BLK), 0)
    qcol = lax.broadcasted_iota(jnp.int32, (BLK, BLK), 1)
    bias_s[0] = jnp.zeros((BLK, BLK), f32)
    bias_s[1] = jnp.where(krow <= qcol, 0.0, LOW).astype(f32)
    bias_s[2] = jnp.full((BLK, BLK), LOW, f32)
    if first:
        m_s[...] = jnp.full(m_s.shape, LOW, f32)
        l_s[...] = jnp.zeros(l_s.shape, f32)
        acc_s[...] = jnp.zeros(acc_s.shape, f32)
    else:
        m_s[...] = carried[0][...]
        l_s[...] = carried[1][...]
        acc_s[...] = carried[2][...]
    p_s[...] = jnp.zeros(p_s.shape, bf16)
    a_s[...] = jnp.ones(a_s.shape, f32)
    group = range(LANES)

    def codes(t):
        out = []
        for a in group:
            code = list_ref[index, t * LANES + a]
            out.append(
                (
                    code & 63,
                    (code >> 4) & 1,
                    ((code >> 8) & 3, (code >> 6) & 3),
                    ((code >> 12) & 3, (code >> 10) & 3),
                    (code >> 14) & 3,
                    (code >> 16) & 3,
                )
            )
        return out

    def value_term(a, item):
        qi, h, k1, k2 = item[:4]
        vt = jnp.concatenate([v_s[k1[0], h, k1[1]], v_s[k2[0], h, k2[1]]], axis=1)
        return acc_s[qi] * a_s[a][:1] + dot1(vt, p_s[a])

    def step(t, carry):
        prev = codes(jnp.maximum(t - 1, 0))
        items = codes(t)
        m_old = [m_s[c[0]] for c in items]
        l_old = [l_s[c[0]] for c in items]

        def score(a):
            qi, h, k1, k2, b1, b2 = items[a]
            qt = q_ref[qi]
            return (
                dot1(k_s[k1[0], h, k1[1]], qt) + bias_s[b1],
                dot1(k_s[k2[0], h, k2[1]], qt) + bias_s[b2],
            )

        ahead = score(0)
        for a in group:
            s1, s2 = ahead
            if a + 1 < LANES:
                ahead = score(a + 1)
            acc = value_term(a, prev[a])
            top = jnp.max(jnp.maximum(s1, s2), axis=0, keepdims=True) * SCALE
            m = jnp.maximum(m_old[a], top)
            alpha = jnp.exp2(m_old[a] - m)
            p1 = jnp.exp2(s1 * SCALE - m[:1])
            p2 = jnp.exp2(s2 * SCALE - m[:1])
            acc_s[prev[a][0]] = acc
            m_s[items[a][0]] = m
            l_s[items[a][0]] = l_old[a] * alpha + jnp.sum(p1 + p2, axis=0, keepdims=True)
            a_s[a] = alpha
            p_s[a] = jnp.concatenate([p1.astype(bf16), p2.astype(bf16)], axis=0)
        return carry

    count = list_ref[index, SLOTS - 1]
    lax.fori_loop(0, count, step, 0)
    prev = codes(jnp.maximum(count - 1, 0))
    for a in group:
        acc_s[prev[a][0]] = value_term(a, prev[a])
    if last:
        sub = lax.broadcasted_iota(jnp.int32, (LSE, BLK), 0)
        for a in range(XN):
            for h in range(HL):
                for i in range(NB):
                    n = (h * XN + a) * NB + i
                    total = l_s[n][:1]
                    some = total > 0.0
                    safe = jnp.where(some, total, 1.0)
                    lse = jnp.where(some, m_s[n][:1] + jnp.log2(safe), LOW)
                    out_ref[a, h * NB + i, :DH] = (acc_s[n] * (1.0 / safe)).astype(bf16)
                    one = lse.astype(bf16).astype(f32)
                    two = (lse - one).astype(bf16).astype(f32)
                    three = (lse - one) - two
                    extra = jnp.where(sub == 0, one, jnp.where(sub == 1, two, jnp.where(sub == 2, three, 0.0)))
                    out_ref[a, h * NB + i, DH:] = extra.astype(bf16)


def combine_kernel(where_ref, *refs):
    parts, weight_ref, out_ref, mixed_ref = refs[:XN], refs[XN], refs[XN + 1], refs[XN + 2]
    y, core = where_ref[2], where_ref[3]
    for i in range(NB):
        mixed = []
        for h in range(HL):
            n = h * NB + i
            rows = []
            for part in parts:
                extra = part[n, DH:].astype(f32)
                rows.append(extra[:1] + extra[1:2] + extra[2:3])
            top = jnp.maximum(jnp.maximum(rows[0], rows[1]), jnp.maximum(rows[2], rows[3]))
            shares = [jnp.exp2(r - top) for r in rows]
            scale = 1.0 / (shares[0] + shares[1] + shares[2] + shares[3])
            acc = parts[0][n, :DH].astype(f32) * (shares[0] * scale)
            for part, share in zip(parts[1:], shares[1:]):
                acc = acc + part[n, :DH].astype(f32) * (share * scale)
            mixed.append(acc.astype(bf16))
        mixed_ref[pl.ds(i * BLK, BLK), :] = jnp.concatenate(mixed, axis=0).T
    for k in range(YN):
        block = weight_ref[((y + k) % YN) * 2 + 1 - core]
        out_ref[k] = dot1(mixed_ref[...], block).astype(bf16)


def own_terms_kernel(where_ref, mixed_ref, weight_ref, out_ref):
    y, core = where_ref[2], where_ref[3]
    for k in range(YN):
        out_ref[k] = dot1(mixed_ref[...], weight_ref[((y + k) % YN) * 2 + core])


def pair_sum_kernel(own_ref, other_ref, keep_ref, *send_refs):
    keep_ref[...] = own_ref[0] + other_ref[0].astype(f32)
    for k, send in enumerate(send_refs):
        send[...] = (own_ref[k + 1] + other_ref[k + 1].astype(f32)).astype(bf16)


def final_sum_kernel(keep_ref, one_ref, two_ref, three_ref, out_ref):
    total = keep_ref[...] + one_ref[...].astype(f32)
    out_ref[...] = (total + (two_ref[...].astype(f32) + three_ref[...].astype(f32))).astype(bf16)


def list_kernel(where_ref, mask_ref, out_ref):
    z, x = where_ref[0], where_ref[1]
    rows = [mask_ref[h, pl.ds(pl.multiple_of(z * XN * NB, XN * NB), XN * NB), :] for h in range(HL)]
    rows = jnp.where(jnp.concatenate(rows * len(CALLS), axis=0) == 1, 1.0, 0.0).astype(bf16)
    slots = XN * NB
    sub = lax.broadcasted_iota(jnp.int32, (slots, BLK), 0)
    lane = lax.broadcasted_iota(jnp.int32, (slots, BLK), 1)
    picked = jnp.zeros((slots, BLK), f32)
    kpos = jnp.full((slots, BLK), -1, jnp.int32)
    for c, js in enumerate(CALLS):
        target = jnp.full((slots, BLK), -1, jnp.int32)
        for r, j in enumerate(js):
            place = (((z - j + ZN) % ZN) * XN + x) * NB + (sub & 3)
            target = jnp.where((sub >> 2) == r, place, target)
        chosen = dot1(jnp.where(lane == target, 1.0, 0.0).astype(bf16), rows, NT)
        picked = jnp.where((lane >> 5) == c, chosen, picked)
        kpos = jnp.where((lane >> 5) == c, target, kpos)
    qpos = z * slots + (lane & 15)
    allowed = (picked > 0.5) & (kpos <= qpos)
    flag = jnp.where(allowed, 1.0, 0.0)
    row16 = lax.broadcasted_iota(jnp.int32, (slots, slots), 0)
    col16 = lax.broadcasted_iota(jnp.int32, (slots, slots), 1)
    earlier = dot1(jnp.where(col16 < row16, 1.0, 0.0).astype(bf16), flag.astype(bf16))
    earlier = jnp.where(allowed, earlier, -1.0)
    value = jnp.where(kpos == qpos, sub + 16, sub).astype(f32)
    total = jnp.sum(flag, axis=0, keepdims=True)
    one = lax.broadcasted_iota(jnp.int32, (1, BLK), 1)
    query = ((one >> 4) & 1) * slots + ((x - ((one >> 2) & 3) + XN) % XN) * NB + (one & 3)
    ranks = 3 * NB // 2

    def nth(p):
        at = jnp.sum(jnp.where(earlier == float(p), value, 0.0), axis=0, keepdims=True)
        return jnp.where(total > float(p), at, 32.0).astype(jnp.int32)

    found = []
    sub8 = lax.broadcasted_iota(jnp.int32, (8, BLK), 0)
    valid = jnp.zeros((8, BLK), f32)
    for p in range(ranks):
        first, second = nth(2 * p), nth(2 * p + 1)
        code = query + ((first & 15) << 6) + ((second & 15) << 10)
        found.append(code + ((first >> 4) << 14) + ((second >> 4) << 16))
        valid = jnp.where((sub8 == p) & (total > float(2 * p)), 1.0, valid)
    ra = lax.broadcasted_iota(jnp.int32, (BLK, BLK), 0)
    ca = lax.broadcasted_iota(jnp.int32, (BLK, BLK), 1)
    same = (ra >> 5) == (ca >> 5)
    valid16 = valid.astype(bf16)
    rank = dot1(valid16, jnp.where(same & (ra < ca), 1.0, 0.0).astype(bf16))
    many = dot1(valid16, jnp.where(same, 1.0, 0.0).astype(bf16))
    used = (many.astype(jnp.int32) + (LANES - 1)) // LANES
    base = jnp.zeros((1, BLK), jnp.int32)
    place = jnp.full((8, BLK), -1.0, f32)
    for p in range(ranks):
        at = base.astype(f32) * float(LANES) + rank
        place = jnp.where((sub8 == p) & (valid > 0.5), at, place)
        base = base + used[p : p + 1]
    ident = jnp.where(ra == ca, 1.0, 0.0).astype(bf16)
    column = dot1(ident, place.astype(bf16), NT)
    spot = lax.broadcasted_iota(jnp.int32, (BLK, SLOTS), 1).astype(f32)
    third = sub // 3
    piece = sub - third * 3
    acc = jnp.zeros((slots, SLOTS), f32)
    for p in range(ranks):
        code = found[p]
        part = jnp.where(piece == 0, code & 255, jnp.where(piece == 1, (code >> 8) & 255, code >> 16))
        part = jnp.where((lane >> 5) == third, part.astype(f32), 0.0)
        part = jnp.where(sub < 12, part, jnp.where((lane >> 5) == sub - 12, 1.0, 0.0))
        hit = jnp.where(column[:, p : p + 1] == spot, 1.0, 0.0).astype(bf16)
        acc = acc + dot1(part.astype(bf16), hit)
    dummy = QB + (2 << 14) + (2 << 16)
    end = lax.broadcasted_iota(jnp.int32, (1, SLOTS), 1)
    for c in range(len(CALLS)):
        low, mid, high = [acc[3 * c + k : 3 * c + k + 1].astype(jnp.int32) for k in range(3)]
        items = low + (mid << 8) + (high << 16)
        items = jnp.where(acc[12 + c : 13 + c] > 0.5, items, dummy)
        count = jnp.max(jnp.where((one >> 5) == c, base, 0), axis=1, keepdims=True)
        out_ref[c : c + 1, :] = jnp.where(end == SLOTS - 1, count, items)


def call(kernel, outs, ins, scratch=(), smem=0, flops=1e9, mib=16):
    size = sum(math.prod(a.shape) * a.dtype.itemsize for a in ins)
    return pl.pallas_call(
        kernel,
        out_shape=outs,
        in_specs=[SMEM] * smem + [VMEM] * (len(ins) - smem),
        out_specs=jax.tree.map(lambda _: VMEM, outs),
        scratch_shapes=list(scratch),
        compiler_params=params(mib),
        cost_estimate=pl.CostEstimate(flops=int(flops), bytes_accessed=size, transcendentals=0),
    )(*ins)


def shape(*dims, dtype=f32):
    return jax.ShapeDtypeStruct(dims, dtype)


def along_z(value, step):
    pairs = [(z * XN + x, ((z + step) % ZN) * XN + x) for z in range(ZN) for x in range(XN)]
    return lax.ppermute(value, "seq", pairs)


def up_z(value, step):
    pairs = [(z * XN + x, (z + step) * XN + x) for z in range(ZN - step) for x in range(XN)]
    return lax.ppermute(value, "seq", pairs)


def along_x(value, step):
    pairs = [(z * XN + x, z * XN + (x + step) % XN) for z in range(ZN) for x in range(XN)]
    return lax.ppermute(value, "seq", pairs)


def sibling(value):
    return lax.ppermute(value, "head", [(g, g ^ 1) for g in range(2 * YN)])


def along_y(value, step):
    pairs = [(g, (g + 2 * step) % (2 * YN)) for g in range(2 * YN)]
    return lax.ppermute(value, "head", pairs)


def ring_z(own):
    rows = [own] + [None] * (ZN - 1)
    for j in range(1, 5):
        rows[j] = along_z(rows[j - 1], 1)
        if j < 4:
            rows[ZN - j] = along_z(rows[(ZN - j + 1) % ZN], -1)
    return rows


def on_device(query, key, value, reflect, block_mask, out_weight):
    here, group = lax.axis_index("seq"), lax.axis_index("head")
    z, x = here // XN, here % XN
    where = jnp.stack([z, x, group // 2, group % 2]).astype(jnp.int32)
    width = out_weight.shape[1] // (2 * YN)
    tokens = query.shape[0]
    tie = lambda *values: lax.optimization_barrier(values)
    square = shape(HL, DH, DH)
    blocks = shape(HL, NB, BLK, DH)
    keys16 = shape(HL, NB, BLK, DH, dtype=bf16)
    v_rows = [value.reshape(NB, BLK, HL, DH).transpose(2, 0, 3, 1)] + [None] * (ZN - 1)
    reflect_h, v_rows[0] = tie(reflect.transpose(1, 0, 2), v_rows[0])
    v_rows[1], v_rows[7] = along_z(v_rows[0], 1), along_z(v_rows[0], -1)
    tri, frames, total = call(
        factor_kernel, (blocks, shape(HL, NB - 1, DH, DH), square), (reflect_h,), flops=2e9
    )
    query, key, block_mask, out_weight, total = tie(query, key, block_mask, out_weight, total)
    others = [along_x(total, k) for k in range(1, XN)]
    q_local, k_local = call(
        local_kernel,
        (blocks, blocks),
        (query.transpose(1, 0, 2), key.transpose(1, 0, 2), reflect_h, tri, frames),
        flops=2e9,
    )
    lists = call(list_kernel, shape(8, SLOTS, dtype=jnp.int32), (where, block_mask), smem=1)
    weight_blocks = out_weight.reshape(-1, 2 * YN, width).transpose(1, 0, 2)
    *others, q_local, k_local, lists, v_rows[1], v_rows[7] = tie(
        *others, q_local, k_local, lists, v_rows[1], v_rows[7]
    )
    before, total = call(
        row_kernel, (shape(XN, HL, DH, DH), square), (where, total, *others), smem=1
    )
    total, q_local, v_rows[1], v_rows[7] = tie(total, q_local, v_rows[1], v_rows[7])
    left = up_z(total, 1)
    q_lanes = [q_local] + [along_x(q_local, k) for k in range(1, XN)]
    v_rows[2], v_rows[6] = along_z(v_rows[1], 1), along_z(v_rows[7], -1)
    left, v_rows[2], v_rows[6] = tie(left, v_rows[2], v_rows[6])
    total, chain = call(partial(hop_kernel, 1), (square, square), (where, left, total), smem=1)
    left = up_z(total, 2)
    v_rows[3], v_rows[5] = along_z(v_rows[2], 1), along_z(v_rows[6], -1)
    left, v_rows[3], v_rows[5] = tie(left, v_rows[3], v_rows[5])
    total, chain = call(
        partial(hop_kernel, 2), (square, square), (where, left, total, chain), smem=1
    )
    left = up_z(total, 4)
    v_rows[4] = along_z(v_rows[5], -1)
    left, weight_blocks, v_rows[4], *q_lanes = tie(left, weight_blocks, v_rows[4], *q_lanes)
    k_turned, chain = call(
        turn_key_kernel, (keys16, square), (where, left, chain, before, k_local), smem=1
    )
    k_rows = ring_z(k_turned)
    queries = call(
        turn_query_kernel, shape(QB + 1, DH, BLK, dtype=bf16), (chain, before, *q_lanes)
    )
    state = (shape(QB + 1, 8, BLK), shape(QB + 1, 8, BLK), shape(QB + 1, DH, BLK))
    carried = ()
    for index, js in enumerate(CALLS):
        last = index == len(CALLS) - 1
        outs = shape(XN, HL * NB, DH + LSE, BLK, dtype=bf16) if last else state
        scratch = [pltpu.VMEM(a.shape, f32) for a in state] if last else []
        scratch += [pltpu.VMEM((len(js), HL, NB, BLK, DH), bf16)] * 2
        scratch += [pltpu.VMEM((3, BLK, BLK), f32), pltpu.VMEM((LANES, 2 * BLK, BLK), bf16)]
        scratch += [pltpu.VMEM((LANES, 8, BLK), f32)]
        carried = call(
            partial(attend_kernel, index, index == 0, last, len(js)),
            outs,
            (lists, queries, *[k_rows[j] for j in js], *[v_rows[j] for j in js], *carried),
            scratch=scratch,
            smem=1,
            flops=2e9 * len(js),
            mib=32,
        )
    got = [carried[0]] + [along_x(carried[a], -a) for a in range(1, XN)]
    sends, mixed = call(
        combine_kernel,
        (shape(YN, tokens, width, dtype=bf16), shape(tokens, HL * DH, dtype=bf16)),
        (where, *got, weight_blocks),
        smem=1,
    )
    other = sibling(sends)
    own = call(own_terms_kernel, shape(YN, tokens, width), (where, mixed, weight_blocks), smem=1)
    part = shape(tokens, width, dtype=bf16)
    keep, *sends = call(
        pair_sum_kernel, (shape(tokens, width), part, part, part), (own, other)
    )
    got = [along_y(sends[k - 1], k) for k in range(1, YN)]
    return call(final_sum_kernel, part, (keep, *got))


def solution(mesh):
    in_specs = (
        P("seq", "head", None),
        P("seq", "head", None),
        P("seq", "head", None),
        P("seq", "head", None),
        P("head", None, None),
        P("head", None),
    )
    out_specs = P("seq", "head")
    return jax.shard_map(
        on_device, mesh=mesh, in_specs=in_specs, out_specs=out_specs, check_vma=False
    )
```

```python
from functools import partial
import math

import jax
import jax.numpy as jnp
from jax import lax
from jax.experimental import pallas as pl
from jax.experimental.pallas import tpu as pltpu
from jax.sharding import PartitionSpec as P

BLK = 128
DH = 128
XN = 4
ZN = 8
HL = 2
NB = 4
YN = 4
QB = HL * XN * NB
LANES = 8
AWAY = QB - HL * NB
LSE = 16
SLOTS = 256
CALLS = ((0, 1, 7), (2, 6), (3, 5), (4,))
EPSILON = 1e-06
LOW = -1e30
SCALE = math.log2(math.e) / math.sqrt(DH)
f32 = jnp.float32
bf16 = jnp.bfloat16
NN = ((1,), (0,))
NT = ((1,), (1,))
TN = ((0,), (0,))
VMEM = pl.BlockSpec(memory_space=pltpu.VMEM)
SMEM = pl.BlockSpec(memory_space=pltpu.SMEM)


def params(mib):
    return pltpu.CompilerParams(vmem_limit_bytes=mib * 1024 * 1024)


def dot1(a, b, dims=NN):
    return lax.dot_general(a, b, (dims, ((), ())), preferred_element_type=f32)


def halves(a):
    high = a.astype(bf16)
    return high, (a - high.astype(f32)).astype(bf16)


def dot3(a, b, dims=NN):
    ah, al = halves(a)
    bh, bl = halves(b)
    return dot1(ah, bh, dims) + (dot1(al, bh, dims) + dot1(ah, bl, dims))


def eye():
    row = lax.broadcasted_iota(jnp.int32, (BLK, BLK), 0)
    col = lax.broadcasted_iota(jnp.int32, (BLK, BLK), 1)
    return jnp.where(row == col, 1.0, 0.0).astype(f32)


def unit_rows(values):
    values = values.astype(f32)
    return values * lax.rsqrt(jnp.sum(values * values, axis=-1, keepdims=True) + EPSILON)


def factor_kernel(reflect_ref, tri_ref, frames_ref, total_ref):
    row = lax.broadcasted_iota(jnp.int32, (BLK, BLK), 0)
    col = lax.broadcasted_iota(jnp.int32, (BLK, BLK), 1)
    ident = jnp.where(row == col, 1.0, 0.0).astype(f32)
    items = [(h, b) for h in range(HL) for b in range(NB)]
    units = [unit_rows(reflect_ref[h, pl.ds(b * BLK, BLK), :]) for h, b in items]
    grams = [2.0 * dot3(u, u, NT) for u in units]
    inv = [ident - jnp.where((row // 2 == col // 2) & (row < col), g, 0.0) for g in grams]
    size = 2
    while size < BLK:
        off = (row // (2 * size) == col // (2 * size)) & (row // size < col // size)
        mids = [dot3(x, jnp.where(off, g, 0.0)) for x, g in zip(inv, grams)]
        inv = [x - dot3(m, x) for x, m in zip(inv, mids)]
        size *= 2
    wholes = []
    for (h, b), u, x in zip(items, units, inv):
        tri = 2.0 * x
        tri_ref[h, b] = tri
        wholes.append(ident - dot3(u, dot3(tri, u), TN))
    frames = [wholes[h * NB] for h in range(HL)]
    for b in range(1, NB):
        for h in range(HL):
            frames_ref[h, b - 1] = frames[h]
        frames = [dot3(frames[h], wholes[h * NB + b]) for h in range(HL)]
    for h in range(HL):
        total_ref[h] = frames[h]


def local_kernel(query_ref, key_ref, reflect_ref, tri_ref, frames_ref, qt_ref, k_ref):
    row = lax.broadcasted_iota(jnp.int32, (2 * BLK, BLK), 0) % BLK
    col = lax.broadcasted_iota(jnp.int32, (2 * BLK, BLK), 1)
    lower = col <= row
    for h in range(HL):
        for b in range(NB):
            here = pl.ds(b * BLK, BLK)
            unit = unit_rows(reflect_ref[h, here, :])
            uh, ul = halves(unit)
            both = jnp.concatenate([query_ref[h, here, :], key_ref[h, here, :]], axis=0)
            proj = dot1(both, uh, NT) + dot1(both, ul, NT)
            coef = dot3(jnp.where(lower, proj, 0.0), tri_ref[h, b], NT)
            turned = both.astype(f32) - dot3(coef, unit)
            if b > 0:
                turned = dot3(turned, frames_ref[h, b - 1], NT)
            qt_ref[h, b] = turned[:BLK].T
            k_ref[h, b] = turned[BLK:]


def row_kernel(where_ref, own_ref, one_ref, two_ref, three_ref, before_ref, total_ref):
    x = where_ref[1]
    for h in range(HL):
        cands = [own_ref[h], one_ref[h], two_ref[h], three_ref[h]]

        def pick(i):
            out = cands[0]
            for k in range(1, XN):
                out = jnp.where((x - k + XN) % XN == i, cands[k], out)
            return out

        first = pick(0)
        second = dot3(first, pick(1))
        third = dot3(second, pick(2))
        for a in range(XN):
            lane = (x - a + XN) % XN
            before = jnp.where(lane == 0, eye(), first)
            before = jnp.where(lane == 2, second, before)
            before_ref[a, h] = jnp.where(lane == 3, third, before)
        total_ref[h] = dot3(third, pick(3))


def hop_kernel(step, where_ref, left_ref, total_ref, *refs):
    z = where_ref[0]
    total_out, chain_out = refs[-2:]
    for h in range(HL):
        left = jnp.where(z >= step, left_ref[h], eye())
        total_out[h] = dot3(left, total_ref[h])
        chain_out[h] = left if step == 1 else dot3(left, refs[0][h])


def turn_key_kernel(where_ref, left_ref, chain_ref, before_ref, k_ref, k_out, chain_out):
    z = where_ref[0]
    for h in range(HL):
        left = jnp.where(z >= 4, left_ref[h], eye())
        chain = dot3(left, chain_ref[h])
        chain_out[h] = chain
        frame = dot3(chain, before_ref[0, h])
        for b in range(NB):
            k_out[h, b] = dot3(k_ref[h, b], frame, NT).astype(bf16)


def turn_query_kernel(chain_ref, before_ref, *refs):
    lanes, out_ref = refs[:XN], refs[XN]
    for a in range(XN):
        for h in range(HL):
            frame = dot3(chain_ref[h], before_ref[a, h])
            for b in range(NB):
                out_ref[(a * HL + h) * NB + b] = dot3(frame, lanes[a][h, b]).astype(bf16)
    out_ref[QB] = jnp.zeros((DH, BLK), bf16)


def attend_kernel(work, offset, first, last, rows, *refs):
    refs = list(refs)
    list_ref, q_ref = refs[:2]
    keys, values = refs[2 : 2 + rows], refs[2 + rows : 2 + 2 * rows]
    refs = refs[2 + 2 * rows :]
    carried = None
    if not first:
        carried, refs = refs[:3], refs[3:]
    if last:
        out_ref, m_s, l_s, acc_s, k_s, v_s, bias_s, p_s, a_s = refs
    else:
        m_s, l_s, acc_s, k_s, v_s, bias_s, p_s, a_s = refs
    for r in range(rows):
        k_s[r] = keys[r][...]
        v_s[r] = values[r][...]
    krow = lax.broadcasted_iota(jnp.int32, (BLK, BLK), 0)
    qcol = lax.broadcasted_iota(jnp.int32, (BLK, BLK), 1)
    bias_s[0] = jnp.zeros((BLK, BLK), f32)
    bias_s[1] = jnp.where(krow <= qcol, 0.0, LOW).astype(f32)
    bias_s[2] = jnp.full((BLK, BLK), LOW, f32)
    if first:
        m_s[...] = jnp.full(m_s.shape, LOW, f32)
        l_s[...] = jnp.zeros(l_s.shape, f32)
        acc_s[...] = jnp.zeros(acc_s.shape, f32)
    else:
        m_s[...] = carried[0][...]
        l_s[...] = carried[1][...]
        acc_s[...] = carried[2][...]
    group = range(LANES)

    for index, base in work:
        p_s[...] = jnp.zeros(p_s.shape, bf16)
        a_s[...] = jnp.ones(a_s.shape, f32)

        def codes(t, index=index, base=base):
            out = []
            for a in group:
                code = list_ref[index, t * LANES + a]
                out.append(
                    (
                        code & 63,
                        (code >> 2) & 1,
                        (((code >> 8) & 3) + base, (code >> 6) & 3),
                        (((code >> 12) & 3) + base, (code >> 10) & 3),
                        (code >> 14) & 3,
                        (code >> 16) & 3,
                    )
                )
            return out

        def value_term(a, item):
            qi, h, k1, k2 = item[:4]
            vt = jnp.concatenate([v_s[k1[0], h, k1[1]], v_s[k2[0], h, k2[1]]], axis=1)
            return acc_s[qi] * a_s[a][:1] + dot1(vt, p_s[a])

        def step(t, carry, codes=codes, value_term=value_term):
            prev = codes(jnp.maximum(t - 1, 0))
            items = codes(t)
            m_old = [m_s[c[0]] for c in items]
            l_old = [l_s[c[0]] for c in items]

            def score(a):
                qi, h, k1, k2, b1, b2 = items[a]
                qt = q_ref[qi + offset]
                return (
                    dot1(k_s[k1[0], h, k1[1]], qt) + bias_s[b1],
                    dot1(k_s[k2[0], h, k2[1]], qt) + bias_s[b2],
                )

            ahead = score(0)
            for a in group:
                s1, s2 = ahead
                if a + 1 < LANES:
                    ahead = score(a + 1)
                acc = value_term(a, prev[a])
                top = jnp.max(jnp.maximum(s1, s2), axis=0, keepdims=True) * SCALE
                m = jnp.maximum(m_old[a], top)
                alpha = jnp.exp2(m_old[a] - m)
                p1 = jnp.exp2(s1 * SCALE - m[:1])
                p2 = jnp.exp2(s2 * SCALE - m[:1])
                acc_s[prev[a][0]] = acc
                m_s[items[a][0]] = m
                l_s[items[a][0]] = l_old[a] * alpha + jnp.sum(p1 + p2, axis=0, keepdims=True)
                a_s[a] = alpha
                p_s[a] = jnp.concatenate([p1.astype(bf16), p2.astype(bf16)], axis=0)
            return carry

        def two_steps(t, carry, step=step):
            return step(2 * t + 1, step(2 * t, carry))

        turns = (list_ref[index, SLOTS - 1] + 1) // 2
        lax.fori_loop(0, turns, two_steps, 0)
        prev = codes(jnp.maximum(2 * turns - 1, 0))
        for a in group:
            acc_s[prev[a][0]] = value_term(a, prev[a])
    if last:
        sub = lax.broadcasted_iota(jnp.int32, (LSE, BLK), 0)
        for n in range(m_s.shape[0] - 1):
            total = l_s[n][:1]
            some = total > 0.0
            safe = jnp.where(some, total, 1.0)
            lse = jnp.where(some, m_s[n][:1] + jnp.log2(safe), LOW)
            out_ref[n // (HL * NB), n % (HL * NB), :DH] = (acc_s[n] * (1.0 / safe)).astype(bf16)
            one = lse.astype(bf16).astype(f32)
            two = (lse - one).astype(bf16).astype(f32)
            three = (lse - one) - two
            extra = jnp.where(sub == 0, one, jnp.where(sub == 1, two, jnp.where(sub == 2, three, 0.0)))
            out_ref[n // (HL * NB), n % (HL * NB), DH:] = extra.astype(bf16)


def weight_block(weight_ref, index):
    width = weight_ref.shape[1] // (2 * YN)
    return weight_ref[:, pl.ds(pl.multiple_of(index * width, width), width)]


def combine_kernel(where_ref, *refs):
    parts, weight_ref, out_ref, mixed_ref = refs[:XN], refs[XN], refs[XN + 1], refs[XN + 2]
    y, core = where_ref[2], where_ref[3]
    for i in range(NB):
        mixed = []
        for h in range(HL):
            n = h * NB + i
            rows = []
            for part in parts:
                extra = part[n, DH:].astype(f32)
                rows.append(extra[:1] + extra[1:2] + extra[2:3])
            top = jnp.maximum(jnp.maximum(rows[0], rows[1]), jnp.maximum(rows[2], rows[3]))
            shares = [jnp.exp2(r - top) for r in rows]
            scale = 1.0 / (shares[0] + shares[1] + shares[2] + shares[3])
            acc = parts[0][n, :DH].astype(f32) * (shares[0] * scale)
            for part, share in zip(parts[1:], shares[1:]):
                acc = acc + part[n, :DH].astype(f32) * (share * scale)
            mixed.append(acc.astype(bf16))
        mixed_ref[pl.ds(i * BLK, BLK), :] = jnp.concatenate(mixed, axis=0).T
    for k in range(YN):
        block = weight_block(weight_ref, ((y + k) % YN) * 2 + 1 - core)
        out_ref[k] = dot1(mixed_ref[...], block).astype(bf16)


def own_terms_kernel(where_ref, mixed_ref, weight_ref, out_ref):
    y, core = where_ref[2], where_ref[3]
    for k in range(YN):
        out_ref[k] = dot1(
            mixed_ref[...], weight_block(weight_ref, ((y + k) % YN) * 2 + core)
        )


def pair_sum_kernel(own_ref, other_ref, keep_ref, *send_refs):
    keep_ref[...] = own_ref[0] + other_ref[0].astype(f32)
    for k, send in enumerate(send_refs):
        send[...] = (own_ref[k + 1] + other_ref[k + 1].astype(f32)).astype(bf16)


def final_sum_kernel(keep_ref, one_ref, two_ref, three_ref, out_ref):
    total = keep_ref[...] + one_ref[...].astype(f32)
    out_ref[...] = (total + (two_ref[...].astype(f32) + three_ref[...].astype(f32))).astype(bf16)


def list_kernel(where_ref, mask_ref, out_ref):
    z, x = where_ref[0], where_ref[1]
    rows = [mask_ref[h, pl.ds(pl.multiple_of(z * XN * NB, XN * NB), XN * NB), :] for h in range(HL)]
    rows = jnp.where(jnp.concatenate(rows * len(CALLS), axis=0) == 1, 1.0, 0.0).astype(bf16)
    slots = XN * NB
    sub = lax.broadcasted_iota(jnp.int32, (slots, BLK), 0)
    lane = lax.broadcasted_iota(jnp.int32, (slots, BLK), 1)
    picked = jnp.zeros((slots, BLK), f32)
    kpos = jnp.full((slots, BLK), -1, jnp.int32)
    for c, js in enumerate(CALLS):
        target = jnp.full((slots, BLK), -1, jnp.int32)
        for r, j in enumerate(js):
            place = (((z - j + ZN) % ZN) * XN + x) * NB + (sub & 3)
            target = jnp.where((sub >> 2) == r, place, target)
        chosen = dot1(jnp.where(lane == target, 1.0, 0.0).astype(bf16), rows, NT)
        picked = jnp.where((lane >> 5) == c, chosen, picked)
        kpos = jnp.where((lane >> 5) == c, target, kpos)
    qpos = z * slots + (lane & 15)
    allowed = (picked > 0.5) & (kpos <= qpos)
    flag = jnp.where(allowed, 1.0, 0.0)
    row16 = lax.broadcasted_iota(jnp.int32, (slots, slots), 0)
    col16 = lax.broadcasted_iota(jnp.int32, (slots, slots), 1)
    earlier = dot1(jnp.where(col16 < row16, 1.0, 0.0).astype(bf16), flag.astype(bf16))
    earlier = jnp.where(allowed, earlier, -1.0)
    value = jnp.where(kpos == qpos, sub + 16, sub).astype(f32)
    total = jnp.sum(flag, axis=0, keepdims=True)
    one = lax.broadcasted_iota(jnp.int32, (1, BLK), 1)
    shift = (x - ((one >> 2) & 3) + XN) % XN
    query = shift * (HL * NB) + ((one >> 4) & 1) * NB + (one & 3)
    ranks = 3 * NB // 2

    def nth(p):
        at = jnp.sum(jnp.where(earlier == float(p), value, 0.0), axis=0, keepdims=True)
        return jnp.where(total > float(p), at, 32.0).astype(jnp.int32)

    pairs = []
    for p in range(ranks):
        first, second = nth(2 * p), nth(2 * p + 1)
        code = ((first & 15) << 6) + ((second & 15) << 10)
        pairs.append(code + ((first >> 4) << 14) + ((second >> 4) << 16))
    sub8 = lax.broadcasted_iota(jnp.int32, (8, BLK), 0)
    ra = lax.broadcasted_iota(jnp.int32, (BLK, BLK), 0)
    ca = lax.broadcasted_iota(jnp.int32, (BLK, BLK), 1)
    same = (ra >> 5) == (ca >> 5)
    below = jnp.where(same & (ra < ca), 1.0, 0.0).astype(bf16)
    within = jnp.where(same, 1.0, 0.0).astype(bf16)
    ident = jnp.where(ra == ca, 1.0, 0.0).astype(bf16)
    spot = lax.broadcasted_iota(jnp.int32, (BLK, SLOTS), 1).astype(f32)
    third = sub // 3
    piece = sub - third * 3
    end = lax.broadcasted_iota(jnp.int32, (1, SLOTS), 1)
    for own in range(2):
        mine = (shift == 0) if own else (shift > 0)
        offset, dummy = (0, HL * NB) if own else (HL * NB, AWAY)
        dummy = dummy + (2 << 14) + (2 << 16)
        valid = jnp.zeros((8, BLK), f32)
        for p in range(ranks):
            valid = jnp.where((sub8 == p) & (total > float(2 * p)) & mine, 1.0, valid)
        valid16 = valid.astype(bf16)
        rank = dot1(valid16, below)
        used = (dot1(valid16, within).astype(jnp.int32) + (LANES - 1)) // LANES
        base = jnp.zeros((1, BLK), jnp.int32)
        place = jnp.full((8, BLK), -1.0, f32)
        for p in range(ranks):
            at = base.astype(f32) * float(LANES) + rank
            place = jnp.where((sub8 == p) & (valid > 0.5), at, place)
            base = base + used[p : p + 1]
        column = dot1(ident, place.astype(bf16), NT)
        acc = jnp.zeros((slots, SLOTS), f32)
        for p in range(ranks):
            code = pairs[p] + (query - offset)
            part = jnp.where(
                piece == 0, code & 255, jnp.where(piece == 1, (code >> 8) & 255, code >> 16)
            )
            part = jnp.where((lane >> 5) == third, part.astype(f32), 0.0)
            part = jnp.where(sub < 12, part, jnp.where((lane >> 5) == sub - 12, 1.0, 0.0))
            hit = jnp.where(column[:, p : p + 1] == spot, 1.0, 0.0).astype(bf16)
            acc = acc + dot1(part.astype(bf16), hit)
        for c in range(len(CALLS)):
            low, mid, high = [acc[3 * c + k : 3 * c + k + 1].astype(jnp.int32) for k in range(3)]
            items = low + (mid << 8) + (high << 16)
            items = jnp.where(acc[12 + c : 13 + c] > 0.5, items, dummy)
            count = jnp.max(jnp.where((one >> 5) == c, base, 0), axis=1, keepdims=True)
            out_ref[4 * own + c : 4 * own + c + 1, :] = jnp.where(end == SLOTS - 1, count, items)


def call(kernel, outs, ins, scratch=(), smem=0, flops=1e9, mib=16):
    size = sum(math.prod(a.shape) * a.dtype.itemsize for a in ins)
    return pl.pallas_call(
        kernel,
        out_shape=outs,
        in_specs=[SMEM] * smem + [VMEM] * (len(ins) - smem),
        out_specs=jax.tree.map(lambda _: VMEM, outs),
        scratch_shapes=list(scratch),
        compiler_params=params(mib),
        cost_estimate=pl.CostEstimate(flops=int(flops), bytes_accessed=size, transcendentals=0),
    )(*ins)


def shape(*dims, dtype=f32):
    return jax.ShapeDtypeStruct(dims, dtype)


def along_z(value, step):
    pairs = [(z * XN + x, ((z + step) % ZN) * XN + x) for z in range(ZN) for x in range(XN)]
    return lax.ppermute(value, "seq", pairs)


def up_z(value, step):
    pairs = [(z * XN + x, (z + step) * XN + x) for z in range(ZN - step) for x in range(XN)]
    return lax.ppermute(value, "seq", pairs)


def along_x(value, step):
    pairs = [(z * XN + x, z * XN + (x + step) % XN) for z in range(ZN) for x in range(XN)]
    return lax.ppermute(value, "seq", pairs)


def sibling(value):
    return lax.ppermute(value, "head", [(g, g ^ 1) for g in range(2 * YN)])


def along_y(value, step):
    pairs = [(g, (g + 2 * step) % (2 * YN)) for g in range(2 * YN)]
    return lax.ppermute(value, "head", pairs)


def on_device(query, key, value, reflect, block_mask, out_weight):
    here, group = lax.axis_index("seq"), lax.axis_index("head")
    z, x = here // XN, here % XN
    where = jnp.stack([z, x, group // 2, group % 2]).astype(jnp.int32)
    width = out_weight.shape[1] // (2 * YN)
    tokens = query.shape[0]
    tie = lambda *values: lax.optimization_barrier(values)
    square = shape(HL, DH, DH)
    blocks = shape(HL, NB, BLK, DH)
    keys16 = shape(HL, NB, BLK, DH, dtype=bf16)
    v_rows = [value.reshape(NB, BLK, HL, DH).transpose(2, 0, 3, 1)] + [None] * (ZN - 1)
    reflect_h = reflect.transpose(1, 0, 2)
    tri, frames, total = call(
        factor_kernel, (blocks, shape(HL, NB - 1, DH, DH), square), (reflect_h,), flops=2e9
    )
    block_mask, v_rows[0], total = tie(block_mask, v_rows[0], total)
    others = [along_x(total, k) for k in range(1, XN)]
    v_rows[1], v_rows[7] = along_z(v_rows[0], 1), along_z(v_rows[0], -1)
    lists = call(list_kernel, shape(8, SLOTS, dtype=jnp.int32), (where, block_mask), smem=1)
    *others, lists = tie(*others, lists)
    before, total = call(
        row_kernel, (shape(XN, HL, DH, DH), square), (where, total, *others), smem=1
    )
    total, query, key = tie(total, query, key)
    left = up_z(total, 1)
    _, v_rows[1], v_rows[7] = tie(total, v_rows[1], v_rows[7])
    v_rows[2], v_rows[6] = along_z(v_rows[1], 1), along_z(v_rows[7], -1)
    q_local, k_local = call(
        local_kernel,
        (blocks, blocks),
        (query.transpose(1, 0, 2), key.transpose(1, 0, 2), reflect_h, tri, frames),
        flops=2e9,
    )
    left, q_local, k_local = tie(left, q_local, k_local)
    total, chain = call(partial(hop_kernel, 1), (square, square), (where, left, total), smem=1)
    total, q_local = tie(total, q_local)
    left = up_z(total, 2)
    q_lanes = [q_local] + [along_x(q_local, k) for k in range(1, XN)]
    total, chain = call(
        partial(hop_kernel, 2), (square, square), (where, left, total, chain), smem=1
    )
    left = up_z(total, 4)
    k_turned, chain = call(
        turn_key_kernel, (keys16, square), (where, left, chain, before, k_local), smem=1
    )
    k_rows = [k_turned, along_z(k_turned, 1)] + [None] * 5 + [along_z(k_turned, -1)]
    queries = call(
        turn_query_kernel, shape(QB + 1, DH, BLK, dtype=bf16), (chain, before, *q_lanes)
    )
    def blank(slots):
        return (shape(slots + 1, 8, BLK), shape(slots + 1, 8, BLK), shape(slots + 1, DH, BLK))

    def attend(work, js, carried, slots, first, last):
        outs = shape(slots // (HL * NB), HL * NB, DH + LSE, BLK, dtype=bf16) if last else blank(slots)
        scratch = [pltpu.VMEM(a.shape, f32) for a in blank(slots)] if last else []
        scratch += [pltpu.VMEM((len(js), HL, NB, BLK, DH), bf16)] * 2
        scratch += [pltpu.VMEM((3, BLK, BLK), f32), pltpu.VMEM((LANES, 2 * BLK, BLK), bf16)]
        scratch += [pltpu.VMEM((LANES, 8, BLK), f32)]
        return call(
            partial(attend_kernel, work, QB - AWAY if slots == AWAY else 0, first, last, len(js)),
            outs,
            (lists, queries, *[k_rows[j] for j in js], *[v_rows[j] for j in js], *carried),
            scratch=scratch,
            smem=1,
            flops=2e9 * len(js),
            mib=16,
        )

    k_rows[1], k_rows[7], queries, v_rows[2], v_rows[6] = tie(
        k_rows[1], k_rows[7], queries, v_rows[2], v_rows[6]
    )
    v_rows[3], v_rows[5] = along_z(v_rows[2], 1), along_z(v_rows[6], -1)
    k_rows[2], k_rows[6] = along_z(k_rows[1], 1), along_z(k_rows[7], -1)
    state = attend(((0, 0),), CALLS[0], (), AWAY, True, False)
    state, k_rows[2], k_rows[6], v_rows[5] = tie(state, k_rows[2], k_rows[6], v_rows[5])
    v_rows[4] = along_z(v_rows[5], -1)
    k_rows[3], k_rows[5] = along_z(k_rows[2], 1), along_z(k_rows[6], -1)
    state = attend(((1, 0),), CALLS[1], state, AWAY, False, False)
    state, queries = tie(state, queries)
    mine = attend(((4, 0), (5, 3)), CALLS[0] + CALLS[1], (), HL * NB, True, False)
    state, mine, k_rows[3], k_rows[5] = tie(state, mine, k_rows[3], k_rows[5])
    k_rows[4] = along_z(k_rows[3], 1)
    state = attend(((2, 0),), CALLS[2], state, AWAY, False, False)
    away = attend(((3, 0),), CALLS[3], state, AWAY, False, True)
    got = [along_x(away[a - 1], -a) for a in range(1, XN)]
    away, mine = tie(away, mine)
    mine = attend(((6, 0), (7, 2)), CALLS[2] + CALLS[3], mine, HL * NB, False, True)
    got = [mine[0]] + got
    sends, mixed = call(
        combine_kernel,
        (shape(YN, tokens, width, dtype=bf16), shape(tokens, HL * DH, dtype=bf16)),
        (where, *got, out_weight),
        smem=1,
    )
    other = sibling(sends)
    own = call(own_terms_kernel, shape(YN, tokens, width), (where, mixed, out_weight), smem=1)
    part = shape(tokens, width, dtype=bf16)
    keep, *sends = call(
        pair_sum_kernel, (shape(tokens, width), part, part, part), (own, other)
    )
    got = [along_y(sends[k - 1], k) for k in range(1, YN)]
    return call(final_sum_kernel, part, (keep, *got))


def solution(mesh):
    in_specs = (
        P("seq", "head", None),
        P("seq", "head", None),
        P("seq", "head", None),
        P("seq", "head", None),
        P("head", None, None),
        P("head", None),
    )
    out_specs = P("seq", "head")
    return jax.shard_map(
        on_device, mesh=mesh, in_specs=in_specs, out_specs=out_specs, check_vma=False
    )
```

```python
from functools import partial
import math

import jax
import jax.numpy as jnp
from jax import lax
from jax.experimental import pallas as pl
from jax.experimental.pallas import tpu as pltpu
from jax.sharding import PartitionSpec as P

BLK = 128
DH = 128
XN = 4
ZN = 8
HL = 2
NB = 4
YN = 4
QB = HL * XN * NB
LANES = 8
AWAY = QB - HL * NB
LSE = 16
SLOTS = 256
CALLS = ((0, 1, 7), (2, 6), (3, 5), (4,))
EPSILON = 1e-06
LOW = -1e30
SCALE = math.log2(math.e) / math.sqrt(DH)
f32 = jnp.float32
bf16 = jnp.bfloat16
NN = ((1,), (0,))
NT = ((1,), (1,))
TN = ((0,), (0,))
VMEM = pl.BlockSpec(memory_space=pltpu.VMEM)
SMEM = pl.BlockSpec(memory_space=pltpu.SMEM)


def params(mib):
    return pltpu.CompilerParams(vmem_limit_bytes=mib * 1024 * 1024)


def dot1(a, b, dims=NN):
    return lax.dot_general(a, b, (dims, ((), ())), preferred_element_type=f32)


def halves(a):
    high = a.astype(bf16)
    return high, (a - high.astype(f32)).astype(bf16)


def dot3(a, b, dims=NN):
    ah, al = halves(a)
    bh, bl = halves(b)
    return dot1(ah, bh, dims) + (dot1(al, bh, dims) + dot1(ah, bl, dims))


def eye():
    row = lax.broadcasted_iota(jnp.int32, (BLK, BLK), 0)
    col = lax.broadcasted_iota(jnp.int32, (BLK, BLK), 1)
    return jnp.where(row == col, 1.0, 0.0).astype(f32)


def unit_rows(values):
    values = values.astype(f32)
    return values * lax.rsqrt(jnp.sum(values * values, axis=-1, keepdims=True) + EPSILON)


def factor_kernel(reflect_ref, tri_ref, frames_ref, total_ref):
    row = lax.broadcasted_iota(jnp.int32, (BLK, BLK), 0)
    col = lax.broadcasted_iota(jnp.int32, (BLK, BLK), 1)
    ident = jnp.where(row == col, 1.0, 0.0).astype(f32)
    items = [(h, b) for h in range(HL) for b in range(NB)]
    units = [unit_rows(reflect_ref[h, pl.ds(b * BLK, BLK), :]) for h, b in items]
    grams = [2.0 * dot3(u, u, NT) for u in units]
    inv = [ident - jnp.where((row // 2 == col // 2) & (row < col), g, 0.0) for g in grams]
    size = 2
    while size < BLK:
        off = (row // (2 * size) == col // (2 * size)) & (row // size < col // size)
        mids = [dot3(x, jnp.where(off, g, 0.0)) for x, g in zip(inv, grams)]
        inv = [x - dot3(m, x) for x, m in zip(inv, mids)]
        size *= 2
    wholes = []
    for (h, b), u, x in zip(items, units, inv):
        tri = 2.0 * x
        tri_ref[h, b] = tri
        wholes.append(ident - dot3(u, dot3(tri, u), TN))
    frames = [wholes[h * NB] for h in range(HL)]
    for b in range(1, NB):
        for h in range(HL):
            frames_ref[h, b - 1] = frames[h]
        frames = [dot3(frames[h], wholes[h * NB + b]) for h in range(HL)]
    for h in range(HL):
        total_ref[h] = frames[h]


def local_kernel(query_ref, key_ref, reflect_ref, tri_ref, frames_ref, qt_ref, k_ref):
    row = lax.broadcasted_iota(jnp.int32, (2 * BLK, BLK), 0) % BLK
    col = lax.broadcasted_iota(jnp.int32, (2 * BLK, BLK), 1)
    lower = col <= row
    for h in range(HL):
        for b in range(NB):
            here = pl.ds(b * BLK, BLK)
            unit = unit_rows(reflect_ref[h, here, :])
            uh, ul = halves(unit)
            both = jnp.concatenate([query_ref[h, here, :], key_ref[h, here, :]], axis=0)
            proj = dot1(both, uh, NT) + dot1(both, ul, NT)
            coef = dot3(jnp.where(lower, proj, 0.0), tri_ref[h, b], NT)
            turned = both.astype(f32) - dot3(coef, unit)
            if b > 0:
                turned = dot3(turned, frames_ref[h, b - 1], NT)
            qt_ref[h, b] = turned[:BLK].T
            k_ref[h, b] = turned[BLK:]


def row_kernel(where_ref, own_ref, one_ref, two_ref, three_ref, before_ref, total_ref):
    x = where_ref[1]
    for h in range(HL):
        cands = [own_ref[h], one_ref[h], two_ref[h], three_ref[h]]

        def pick(i):
            out = cands[0]
            for k in range(1, XN):
                out = jnp.where((x - k + XN) % XN == i, cands[k], out)
            return out

        first = pick(0)
        second = dot3(first, pick(1))
        third = dot3(second, pick(2))
        before = jnp.where(x == 0, eye(), first)
        before = jnp.where(x == 2, second, before)
        before_ref[h] = jnp.where(x == 3, third, before)
        total_ref[h] = dot3(third, pick(3))


def hop_kernel(step, where_ref, left_ref, total_ref, *refs):
    z = where_ref[0]
    total_out, chain_out = refs[-2:]
    for h in range(HL):
        left = jnp.where(z >= step, left_ref[h], eye())
        total_out[h] = dot3(left, total_ref[h])
        chain_out[h] = left if step == 1 else dot3(left, refs[0][h])


def turn_kernel(where_ref, left_ref, chain_ref, before_ref, qt_ref, k_ref, k_out, qt_out):
    z = where_ref[0]
    for h in range(HL):
        left = jnp.where(z >= 4, left_ref[h], eye())
        frame = dot3(left, dot3(chain_ref[h], before_ref[h]))
        for b in range(NB):
            k_out[h, b] = dot3(k_ref[h, b], frame, NT).astype(bf16)
            qt_out[h, b] = dot3(frame, qt_ref[h, b]).astype(bf16)


def attend_kernel(work, lanes, first, last, rows, *refs):
    refs = list(refs)
    list_ref, queries, refs = refs[0], refs[1 : 1 + lanes], refs[1 + lanes :]
    keys, values = refs[:rows], refs[rows : 2 * rows]
    refs = refs[2 * rows :]
    carried = None
    if not first:
        carried, refs = refs[:3], refs[3:]
    if last:
        out_ref, m_s, l_s, acc_s, q_s, k_s, v_s, bias_s, p_s, a_s = refs
    else:
        m_s, l_s, acc_s, q_s, k_s, v_s, bias_s, p_s, a_s = refs
    for r in range(rows):
        k_s[r] = keys[r][...]
        v_s[r] = values[r][...]
    for a in range(lanes):
        for h in range(HL):
            for i in range(NB):
                q_s[(a * HL + h) * NB + i] = queries[a][h, i]
    q_s[lanes * HL * NB] = jnp.zeros((DH, BLK), bf16)
    krow = lax.broadcasted_iota(jnp.int32, (BLK, BLK), 0)
    qcol = lax.broadcasted_iota(jnp.int32, (BLK, BLK), 1)
    bias_s[0] = jnp.zeros((BLK, BLK), f32)
    bias_s[1] = jnp.where(krow <= qcol, 0.0, LOW).astype(f32)
    bias_s[2] = jnp.full((BLK, BLK), LOW, f32)
    if first:
        m_s[...] = jnp.full(m_s.shape, LOW, f32)
        l_s[...] = jnp.zeros(l_s.shape, f32)
        acc_s[...] = jnp.zeros(acc_s.shape, f32)
    else:
        m_s[...] = carried[0][...]
        l_s[...] = carried[1][...]
        acc_s[...] = carried[2][...]
    group = range(LANES)

    for index, base in work:
        p_s[...] = jnp.zeros(p_s.shape, bf16)
        a_s[...] = jnp.ones(a_s.shape, f32)

        def codes(t, index=index, base=base):
            out = []
            for a in group:
                code = list_ref[index, t * LANES + a]
                out.append(
                    (
                        code & 63,
                        (code >> 2) & 1,
                        (((code >> 8) & 3) + base, (code >> 6) & 3),
                        (((code >> 12) & 3) + base, (code >> 10) & 3),
                        (code >> 14) & 3,
                        (code >> 16) & 3,
                    )
                )
            return out

        def value_term(a, item):
            qi, h, k1, k2 = item[:4]
            vt = jnp.concatenate([v_s[k1[0], h, k1[1]], v_s[k2[0], h, k2[1]]], axis=1)
            return acc_s[qi] * a_s[a][:1] + dot1(vt, p_s[a])

        def step(t, carry, codes=codes, value_term=value_term):
            prev = codes(jnp.maximum(t - 1, 0))
            items = codes(t)
            m_old = [m_s[c[0]] for c in items]
            l_old = [l_s[c[0]] for c in items]

            def score(a):
                qi, h, k1, k2, b1, b2 = items[a]
                qt = q_s[qi]
                return (
                    dot1(k_s[k1[0], h, k1[1]], qt) + bias_s[b1],
                    dot1(k_s[k2[0], h, k2[1]], qt) + bias_s[b2],
                )

            ahead = score(0)
            for a in group:
                s1, s2 = ahead
                if a + 1 < LANES:
                    ahead = score(a + 1)
                acc = value_term(a, prev[a])
                top = jnp.max(jnp.maximum(s1, s2), axis=0, keepdims=True) * SCALE
                m = jnp.maximum(m_old[a], top)
                alpha = jnp.exp2(m_old[a] - m)
                p1 = jnp.exp2(s1 * SCALE - m[:1])
                p2 = jnp.exp2(s2 * SCALE - m[:1])
                acc_s[prev[a][0]] = acc
                m_s[items[a][0]] = m
                l_s[items[a][0]] = l_old[a] * alpha + jnp.sum(p1 + p2, axis=0, keepdims=True)
                a_s[a] = alpha
                p_s[a] = jnp.concatenate([p1.astype(bf16), p2.astype(bf16)], axis=0)
            return carry

        def two_steps(t, carry, step=step):
            return step(2 * t + 1, step(2 * t, carry))

        turns = (list_ref[index, SLOTS - 1] + 1) // 2
        lax.fori_loop(0, turns, two_steps, 0)
        prev = codes(jnp.maximum(2 * turns - 1, 0))
        for a in group:
            acc_s[prev[a][0]] = value_term(a, prev[a])
    if last:
        sub = lax.broadcasted_iota(jnp.int32, (LSE, BLK), 0)
        for n in range(m_s.shape[0] - 1):
            total = l_s[n][:1]
            some = total > 0.0
            safe = jnp.where(some, total, 1.0)
            lse = jnp.where(some, m_s[n][:1] + jnp.log2(safe), LOW)
            out_ref[n // (HL * NB), n % (HL * NB), :DH] = (acc_s[n] * (1.0 / safe)).astype(bf16)
            one = lse.astype(bf16).astype(f32)
            two = (lse - one).astype(bf16).astype(f32)
            three = (lse - one) - two
            extra = jnp.where(sub == 0, one, jnp.where(sub == 1, two, jnp.where(sub == 2, three, 0.0)))
            out_ref[n // (HL * NB), n % (HL * NB), DH:] = extra.astype(bf16)


def weight_block(weight_ref, index):
    width = weight_ref.shape[1] // (2 * YN)
    return weight_ref[:, pl.ds(pl.multiple_of(index * width, width), width)]


def combine_kernel(where_ref, *refs):
    parts, weight_ref, out_ref, mixed_ref = refs[:XN], refs[XN], refs[XN + 1], refs[XN + 2]
    y, core = where_ref[2], where_ref[3]
    for i in range(NB):
        mixed = []
        for h in range(HL):
            n = h * NB + i
            rows = []
            for part in parts:
                extra = part[n, DH:].astype(f32)
                rows.append(extra[:1] + extra[1:2] + extra[2:3])
            top = jnp.maximum(jnp.maximum(rows[0], rows[1]), jnp.maximum(rows[2], rows[3]))
            shares = [jnp.exp2(r - top) for r in rows]
            scale = 1.0 / (shares[0] + shares[1] + shares[2] + shares[3])
            acc = parts[0][n, :DH].astype(f32) * (shares[0] * scale)
            for part, share in zip(parts[1:], shares[1:]):
                acc = acc + part[n, :DH].astype(f32) * (share * scale)
            mixed.append(acc.astype(bf16))
        mixed_ref[pl.ds(i * BLK, BLK), :] = jnp.concatenate(mixed, axis=0).T
    for k in range(YN):
        block = weight_block(weight_ref, ((y + k) % YN) * 2 + 1 - core)
        out_ref[k] = dot1(mixed_ref[...], block).astype(bf16)


def own_terms_kernel(where_ref, mixed_ref, weight_ref, out_ref):
    y, core = where_ref[2], where_ref[3]
    for k in range(YN):
        out_ref[k] = dot1(
            mixed_ref[...], weight_block(weight_ref, ((y + k) % YN) * 2 + core)
        )


def pair_sum_kernel(own_ref, other_ref, keep_ref, *send_refs):
    keep_ref[...] = own_ref[0] + other_ref[0].astype(f32)
    for k, send in enumerate(send_refs):
        send[...] = (own_ref[k + 1] + other_ref[k + 1].astype(f32)).astype(bf16)


def final_sum_kernel(keep_ref, one_ref, two_ref, three_ref, out_ref):
    total = keep_ref[...] + one_ref[...].astype(f32)
    out_ref[...] = (total + (two_ref[...].astype(f32) + three_ref[...].astype(f32))).astype(bf16)


def list_kernel(where_ref, mask_ref, out_ref):
    z, x = where_ref[0], where_ref[1]
    rows = [mask_ref[h, pl.ds(pl.multiple_of(z * XN * NB, XN * NB), XN * NB), :] for h in range(HL)]
    rows = jnp.where(jnp.concatenate(rows * len(CALLS), axis=0) == 1, 1.0, 0.0).astype(bf16)
    slots = XN * NB
    sub = lax.broadcasted_iota(jnp.int32, (slots, BLK), 0)
    lane = lax.broadcasted_iota(jnp.int32, (slots, BLK), 1)
    picked = jnp.zeros((slots, BLK), f32)
    kpos = jnp.full((slots, BLK), -1, jnp.int32)
    for c, js in enumerate(CALLS):
        target = jnp.full((slots, BLK), -1, jnp.int32)
        for r, j in enumerate(js):
            place = (((z - j + ZN) % ZN) * XN + x) * NB + (sub & 3)
            target = jnp.where((sub >> 2) == r, place, target)
        chosen = dot1(jnp.where(lane == target, 1.0, 0.0).astype(bf16), rows, NT)
        picked = jnp.where((lane >> 5) == c, chosen, picked)
        kpos = jnp.where((lane >> 5) == c, target, kpos)
    qpos = z * slots + (lane & 15)
    allowed = (picked > 0.5) & (kpos <= qpos)
    flag = jnp.where(allowed, 1.0, 0.0)
    row16 = lax.broadcasted_iota(jnp.int32, (slots, slots), 0)
    col16 = lax.broadcasted_iota(jnp.int32, (slots, slots), 1)
    earlier = dot1(jnp.where(col16 < row16, 1.0, 0.0).astype(bf16), flag.astype(bf16))
    earlier = jnp.where(allowed, earlier, -1.0)
    value = jnp.where(kpos == qpos, sub + 16, sub).astype(f32)
    total = jnp.sum(flag, axis=0, keepdims=True)
    one = lax.broadcasted_iota(jnp.int32, (1, BLK), 1)
    shift = (x - ((one >> 2) & 3) + XN) % XN
    query = shift * (HL * NB) + ((one >> 4) & 1) * NB + (one & 3)
    ranks = 3 * NB // 2

    def nth(p):
        at = jnp.sum(jnp.where(earlier == float(p), value, 0.0), axis=0, keepdims=True)
        return jnp.where(total > float(p), at, 32.0).astype(jnp.int32)

    pairs = []
    for p in range(ranks):
        first, second = nth(2 * p), nth(2 * p + 1)
        code = ((first & 15) << 6) + ((second & 15) << 10)
        pairs.append(code + ((first >> 4) << 14) + ((second >> 4) << 16))
    sub8 = lax.broadcasted_iota(jnp.int32, (8, BLK), 0)
    ra = lax.broadcasted_iota(jnp.int32, (BLK, BLK), 0)
    ca = lax.broadcasted_iota(jnp.int32, (BLK, BLK), 1)
    same = (ra >> 5) == (ca >> 5)
    below = jnp.where(same & (ra < ca), 1.0, 0.0).astype(bf16)
    within = jnp.where(same, 1.0, 0.0).astype(bf16)
    ident = jnp.where(ra == ca, 1.0, 0.0).astype(bf16)
    spot = lax.broadcasted_iota(jnp.int32, (BLK, SLOTS), 1).astype(f32)
    third = sub // 3
    piece = sub - third * 3
    end = lax.broadcasted_iota(jnp.int32, (1, SLOTS), 1)
    for own in range(2):
        mine = (shift == 0) if own else (shift > 0)
        offset, dummy = (0, HL * NB) if own else (HL * NB, AWAY)
        dummy = dummy + (2 << 14) + (2 << 16)
        valid = jnp.zeros((8, BLK), f32)
        for p in range(ranks):
            valid = jnp.where((sub8 == p) & (total > float(2 * p)) & mine, 1.0, valid)
        valid16 = valid.astype(bf16)
        rank = dot1(valid16, below)
        used = (dot1(valid16, within).astype(jnp.int32) + (LANES - 1)) // LANES
        base = jnp.zeros((1, BLK), jnp.int32)
        place = jnp.full((8, BLK), -1.0, f32)
        for p in range(ranks):
            at = base.astype(f32) * float(LANES) + rank
            place = jnp.where((sub8 == p) & (valid > 0.5), at, place)
            base = base + used[p : p + 1]
        column = dot1(ident, place.astype(bf16), NT)
        acc = jnp.zeros((slots, SLOTS), f32)
        for p in range(ranks):
            code = pairs[p] + (query - offset)
            part = jnp.where(
                piece == 0, code & 255, jnp.where(piece == 1, (code >> 8) & 255, code >> 16)
            )
            part = jnp.where((lane >> 5) == third, part.astype(f32), 0.0)
            part = jnp.where(sub < 12, part, jnp.where((lane >> 5) == sub - 12, 1.0, 0.0))
            hit = jnp.where(column[:, p : p + 1] == spot, 1.0, 0.0).astype(bf16)
            acc = acc + dot1(part.astype(bf16), hit)
        for c in range(len(CALLS)):
            low, mid, high = [acc[3 * c + k : 3 * c + k + 1].astype(jnp.int32) for k in range(3)]
            items = low + (mid << 8) + (high << 16)
            items = jnp.where(acc[12 + c : 13 + c] > 0.5, items, dummy)
            count = jnp.max(jnp.where((one >> 5) == c, base, 0), axis=1, keepdims=True)
            out_ref[4 * own + c : 4 * own + c + 1, :] = jnp.where(end == SLOTS - 1, count, items)


def call(kernel, outs, ins, scratch=(), smem=0, flops=1e9, mib=16):
    size = sum(math.prod(a.shape) * a.dtype.itemsize for a in ins)
    return pl.pallas_call(
        kernel,
        out_shape=outs,
        in_specs=[SMEM] * smem + [VMEM] * (len(ins) - smem),
        out_specs=jax.tree.map(lambda _: VMEM, outs),
        scratch_shapes=list(scratch),
        compiler_params=params(mib),
        cost_estimate=pl.CostEstimate(flops=int(flops), bytes_accessed=size, transcendentals=0),
    )(*ins)


def shape(*dims, dtype=f32):
    return jax.ShapeDtypeStruct(dims, dtype)


def along_z(value, step):
    pairs = [(z * XN + x, ((z + step) % ZN) * XN + x) for z in range(ZN) for x in range(XN)]
    return lax.ppermute(value, "seq", pairs)


def up_z(value, step):
    pairs = [(z * XN + x, (z + step) * XN + x) for z in range(ZN - step) for x in range(XN)]
    return lax.ppermute(value, "seq", pairs)


def along_x(value, step):
    pairs = [(z * XN + x, z * XN + (x + step) % XN) for z in range(ZN) for x in range(XN)]
    return lax.ppermute(value, "seq", pairs)


def sibling(value):
    return lax.ppermute(value, "head", [(g, g ^ 1) for g in range(2 * YN)])


def along_y(value, step):
    pairs = [(g, (g + 2 * step) % (2 * YN)) for g in range(2 * YN)]
    return lax.ppermute(value, "head", pairs)


def on_device(query, key, value, reflect, block_mask, out_weight):
    here, group = lax.axis_index("seq"), lax.axis_index("head")
    z, x = here // XN, here % XN
    where = jnp.stack([z, x, group // 2, group % 2]).astype(jnp.int32)
    width = out_weight.shape[1] // (2 * YN)
    tokens = query.shape[0]
    tie = lambda *values: lax.optimization_barrier(values)
    square = shape(HL, DH, DH)
    blocks = shape(HL, NB, BLK, DH)
    keys16 = shape(HL, NB, BLK, DH, dtype=bf16)
    v_rows = [value.reshape(NB, BLK, HL, DH).transpose(2, 0, 3, 1)] + [None] * (ZN - 1)
    reflect_h = reflect.transpose(1, 0, 2)
    tri, frames, total = call(
        factor_kernel, (blocks, shape(HL, NB - 1, DH, DH), square), (reflect_h,), flops=2e9
    )
    block_mask, v_rows[0], total = tie(block_mask, v_rows[0], total)
    others = [along_x(total, k) for k in range(1, XN)]
    v_rows[1], v_rows[7] = along_z(v_rows[0], 1), along_z(v_rows[0], -1)
    lists = call(list_kernel, shape(8, SLOTS, dtype=jnp.int32), (where, block_mask), smem=1)
    *others, lists = tie(*others, lists)
    before, total = call(
        row_kernel, (square, square), (where, total, *others), smem=1
    )
    total, query, key = tie(total, query, key)
    left = up_z(total, 1)
    _, v_rows[7] = tie(total, v_rows[7])
    v_rows[6] = along_z(v_rows[7], -1)
    q_local, k_local = call(
        local_kernel,
        (blocks, blocks),
        (query.transpose(1, 0, 2), key.transpose(1, 0, 2), reflect_h, tri, frames),
        flops=2e9,
    )
    left, q_local, k_local, v_rows[1] = tie(left, q_local, k_local, v_rows[1])
    total, chain = call(partial(hop_kernel, 1), (square, square), (where, left, total), smem=1)
    left = up_z(total, 2)
    _, v_rows[6] = tie(total, v_rows[6])
    v_rows[5] = along_z(v_rows[6], -1)
    total, chain = call(
        partial(hop_kernel, 2), (square, square), (where, left, total, chain), smem=1
    )
    left = up_z(total, 4)
    _, v_rows[5] = tie(total, v_rows[5])
    v_rows[4] = along_z(v_rows[5], -1)
    k_turned, q_turned = call(
        turn_kernel, (keys16, keys16), (where, left, chain, before, q_local, k_local), smem=1
    )
    k_rows = [k_turned, along_z(k_turned, 1)] + [None] * 5 + [along_z(k_turned, -1)]
    lanes = [along_x(q_turned, k) for k in range(1, XN)]
    _, v_rows[1] = tie(k_turned, v_rows[1])
    v_rows[2] = along_z(v_rows[1], 1)

    def blank(slots):
        return (shape(slots + 1, 8, BLK), shape(slots + 1, 8, BLK), shape(slots + 1, DH, BLK))

    def attend(work, js, carried, slots, first, last):
        queries = lanes if slots == AWAY else [q_turned]
        outs = shape(slots // (HL * NB), HL * NB, DH + LSE, BLK, dtype=bf16) if last else blank(slots)
        scratch = [pltpu.VMEM(a.shape, f32) for a in blank(slots)] if last else []
        scratch += [pltpu.VMEM((slots + 1, DH, BLK), bf16)]
        scratch += [pltpu.VMEM((len(js), HL, NB, BLK, DH), bf16)] * 2
        scratch += [pltpu.VMEM((3, BLK, BLK), f32), pltpu.VMEM((LANES, 2 * BLK, BLK), bf16)]
        scratch += [pltpu.VMEM((LANES, 8, BLK), f32)]
        return call(
            partial(attend_kernel, work, len(queries), first, last, len(js)),
            outs,
            (lists, *queries, *[k_rows[j] for j in js], *[v_rows[j] for j in js], *carried),
            scratch=scratch,
            smem=1,
            flops=2e9 * len(js),
            mib=16,
        )

    k_rows[1], k_rows[7], v_rows[2] = tie(k_rows[1], k_rows[7], v_rows[2])
    v_rows[3] = along_z(v_rows[2], 1)
    k_rows[2], k_rows[6] = along_z(k_rows[1], 1), along_z(k_rows[7], -1)
    state = attend(((0, 0),), CALLS[0], (), AWAY, True, False)
    state, k_rows[2], k_rows[6] = tie(state, k_rows[2], k_rows[6])
    k_rows[3], k_rows[5] = along_z(k_rows[2], 1), along_z(k_rows[6], -1)
    state = attend(((1, 0),), CALLS[1], state, AWAY, False, False)
    state, q_turned = tie(state, q_turned)
    mine = attend(((4, 0), (5, 3)), CALLS[0] + CALLS[1], (), HL * NB, True, False)
    state, mine, k_rows[3], k_rows[5] = tie(state, mine, k_rows[3], k_rows[5])
    k_rows[4] = along_z(k_rows[3], 1)
    state = attend(((2, 0),), CALLS[2], state, AWAY, False, False)
    away = attend(((3, 0),), CALLS[3], state, AWAY, False, True)
    got = [along_x(away[a - 1], -a) for a in range(1, XN)]
    away, mine = tie(away, mine)
    mine = attend(((6, 0), (7, 2)), CALLS[2] + CALLS[3], mine, HL * NB, False, True)
    got = [mine[0]] + got
    sends, mixed = call(
        combine_kernel,
        (shape(YN, tokens, width, dtype=bf16), shape(tokens, HL * DH, dtype=bf16)),
        (where, *got, out_weight),
        smem=1,
    )
    other = sibling(sends)
    own = call(own_terms_kernel, shape(YN, tokens, width), (where, mixed, out_weight), smem=1)
    part = shape(tokens, width, dtype=bf16)
    keep, *sends = call(
        pair_sum_kernel, (shape(tokens, width), part, part, part), (own, other)
    )
    got = [along_y(sends[k - 1], k) for k in range(1, YN)]
    return call(final_sum_kernel, part, (keep, *got))


def solution(mesh):
    in_specs = (
        P("seq", "head", None),
        P("seq", "head", None),
        P("seq", "head", None),
        P("seq", "head", None),
        P("head", None, None),
        P("head", None),
    )
    out_specs = P("seq", "head")
    return jax.shard_map(
        on_device, mesh=mesh, in_specs=in_specs, out_specs=out_specs, check_vma=False
    )
```

```python
from functools import partial
import math

import jax
import jax.numpy as jnp
from jax import lax
from jax.experimental import pallas as pl
from jax.experimental.pallas import tpu as pltpu
from jax.sharding import PartitionSpec as P

BLK = 128
DH = 128
XN = 4
ZN = 8
HL = 2
NB = 4
YN = 4
QB = HL * XN * NB
LANES = 8
AWAY = QB - HL * NB
LSE = 16
SLOTS = 256
CALLS = ((0, 1, 7), (2, 6), (3, 5), (4,))
EPSILON = 1e-06
LOW = -1e30
SCALE = math.log2(math.e) / math.sqrt(DH)
f32 = jnp.float32
bf16 = jnp.bfloat16
NN = ((1,), (0,))
NT = ((1,), (1,))
TN = ((0,), (0,))
VMEM = pl.BlockSpec(memory_space=pltpu.VMEM)
SMEM = pl.BlockSpec(memory_space=pltpu.SMEM)


def params(mib):
    return pltpu.CompilerParams(vmem_limit_bytes=mib * 1024 * 1024)


def dot1(a, b, dims=NN):
    return lax.dot_general(a, b, (dims, ((), ())), preferred_element_type=f32)


def halves(a):
    high = a.astype(bf16)
    return high, (a - high.astype(f32)).astype(bf16)


def dot3(a, b, dims=NN):
    ah, al = halves(a)
    bh, bl = halves(b)
    return dot1(ah, bh, dims) + (dot1(al, bh, dims) + dot1(ah, bl, dims))


def eye():
    row = lax.broadcasted_iota(jnp.int32, (BLK, BLK), 0)
    col = lax.broadcasted_iota(jnp.int32, (BLK, BLK), 1)
    return jnp.where(row == col, 1.0, 0.0).astype(f32)


def unit_rows(values):
    values = values.astype(f32)
    return values * lax.rsqrt(jnp.sum(values * values, axis=-1, keepdims=True) + EPSILON)


def factor_kernel(reflect_ref, tri_ref, frames_ref, total_ref):
    row = lax.broadcasted_iota(jnp.int32, (BLK, BLK), 0)
    col = lax.broadcasted_iota(jnp.int32, (BLK, BLK), 1)
    ident = jnp.where(row == col, 1.0, 0.0).astype(f32)
    items = [(h, b) for h in range(HL) for b in range(NB)]
    units = [unit_rows(reflect_ref[h, pl.ds(b * BLK, BLK), :]) for h, b in items]
    grams = [2.0 * dot3(u, u, NT) for u in units]
    inv = [ident - jnp.where((row // 2 == col // 2) & (row < col), g, 0.0) for g in grams]
    size = 2
    while size < BLK:
        off = (row // (2 * size) == col // (2 * size)) & (row // size < col // size)
        mids = [dot3(x, jnp.where(off, g, 0.0)) for x, g in zip(inv, grams)]
        inv = [x - dot3(m, x) for x, m in zip(inv, mids)]
        size *= 2
    wholes = []
    for (h, b), u, x in zip(items, units, inv):
        tri = 2.0 * x
        tri_ref[h, b] = tri
        wholes.append(ident - dot3(u, dot3(tri, u), TN))
    frames = [wholes[h * NB] for h in range(HL)]
    for b in range(1, NB):
        for h in range(HL):
            frames_ref[h, b - 1] = frames[h]
        frames = [dot3(frames[h], wholes[h * NB + b]) for h in range(HL)]
    for h in range(HL):
        total_ref[h] = frames[h]


def local_kernel(query_ref, key_ref, reflect_ref, tri_ref, frames_ref, qt_ref, k_ref):
    row = lax.broadcasted_iota(jnp.int32, (2 * BLK, BLK), 0) % BLK
    col = lax.broadcasted_iota(jnp.int32, (2 * BLK, BLK), 1)
    lower = col <= row
    for h in range(HL):
        for b in range(NB):
            here = pl.ds(b * BLK, BLK)
            unit = unit_rows(reflect_ref[h, here, :])
            uh, ul = halves(unit)
            both = jnp.concatenate([query_ref[h, here, :], key_ref[h, here, :]], axis=0)
            proj = dot1(both, uh, NT) + dot1(both, ul, NT)
            coef = dot3(jnp.where(lower, proj, 0.0), tri_ref[h, b], NT)
            turned = both.astype(f32) - dot3(coef, unit)
            if b > 0:
                turned = dot3(turned, frames_ref[h, b - 1], NT)
            qt_ref[h, b] = turned[:BLK].T
            k_ref[h, b] = turned[BLK:]


def row_kernel(where_ref, own_ref, one_ref, two_ref, three_ref, before_ref, total_ref):
    x = where_ref[1]
    for h in range(HL):
        cands = [own_ref[h], one_ref[h], two_ref[h], three_ref[h]]

        def pick(i):
            out = cands[0]
            for k in range(1, XN):
                out = jnp.where((x - k + XN) % XN == i, cands[k], out)
            return out

        first = pick(0)
        second = dot3(first, pick(1))
        third = dot3(second, pick(2))
        before = jnp.where(x == 0, eye(), first)
        before = jnp.where(x == 2, second, before)
        before_ref[h] = jnp.where(x == 3, third, before)
        total_ref[h] = dot3(third, pick(3))


def hop_kernel(step, where_ref, left_ref, total_ref, *refs):
    z = where_ref[0]
    total_out, chain_out = refs[-2:]
    for h in range(HL):
        left = jnp.where(z >= step, left_ref[h], eye())
        total_out[h] = dot3(left, total_ref[h])
        chain_out[h] = left if step == 1 else dot3(left, refs[0][h])


def turn_kernel(where_ref, left_ref, chain_ref, before_ref, qt_ref, k_ref, k_out, qt_out):
    z = where_ref[0]
    for h in range(HL):
        left = jnp.where(z >= 4, left_ref[h], eye())
        frame = dot3(left, dot3(chain_ref[h], before_ref[h]))
        for b in range(NB):
            k_out[h, b] = dot3(k_ref[h, b], frame, NT).astype(bf16)
            qt_out[h, b] = dot3(frame, qt_ref[h, b]).astype(bf16)


def attend_kernel(work, lanes, first, last, rows, *refs):
    refs = list(refs)
    list_ref, queries, refs = refs[0], refs[1 : 1 + lanes], refs[1 + lanes :]
    keys, values = refs[:rows], refs[rows : 2 * rows]
    refs = refs[2 * rows :]
    carried = None
    if not first:
        carried, refs = refs[:3], refs[3:]
    if last:
        out_ref, m_s, l_s, acc_s, q_s, k_s, v_s, bias_s, p_s, a_s = refs
    else:
        m_s, l_s, acc_s, q_s, k_s, v_s, bias_s, p_s, a_s = refs
    for r in range(rows):
        k_s[r] = keys[r][...]
        v_s[r] = values[r][...]
    for a in range(lanes):
        for h in range(HL):
            for i in range(NB):
                q_s[(a * HL + h) * NB + i] = queries[a][h, i]
    q_s[lanes * HL * NB] = jnp.zeros((DH, BLK), bf16)
    krow = lax.broadcasted_iota(jnp.int32, (BLK, BLK), 0)
    qcol = lax.broadcasted_iota(jnp.int32, (BLK, BLK), 1)
    bias_s[0] = jnp.zeros((BLK, BLK), f32)
    bias_s[1] = jnp.where(krow <= qcol, 0.0, LOW).astype(f32)
    bias_s[2] = jnp.full((BLK, BLK), LOW, f32)
    if first:
        m_s[...] = jnp.full(m_s.shape, LOW, f32)
        l_s[...] = jnp.zeros(l_s.shape, f32)
        acc_s[...] = jnp.zeros(acc_s.shape, f32)
    else:
        m_s[...] = carried[0][...]
        l_s[...] = carried[1][...]
        acc_s[...] = carried[2][...]
    group = range(LANES)

    for index, base in work:
        p_s[...] = jnp.zeros(p_s.shape, bf16)
        a_s[...] = jnp.ones(a_s.shape, f32)

        def codes(t, index=index, base=base):
            out = []
            for a in group:
                code = list_ref[index, t * LANES + a]
                out.append(
                    (
                        code & 63,
                        (code >> 2) & 1,
                        (((code >> 8) & 3) + base, (code >> 6) & 3),
                        (((code >> 12) & 3) + base, (code >> 10) & 3),
                        (code >> 14) & 3,
                        (code >> 16) & 3,
                    )
                )
            return out

        def value_term(a, item):
            qi, h, k1, k2 = item[:4]
            vt = jnp.concatenate([v_s[k1[0], h, k1[1]], v_s[k2[0], h, k2[1]]], axis=1)
            return acc_s[qi] * a_s[a][:1] + dot1(vt, p_s[a])

        def step(t, carry, codes=codes, value_term=value_term):
            prev = codes(jnp.maximum(t - 1, 0))
            items = codes(t)
            m_old = [m_s[c[0]] for c in items]
            l_old = [l_s[c[0]] for c in items]

            def score(a):
                qi, h, k1, k2, b1, b2 = items[a]
                qt = q_s[qi]
                return (
                    dot1(k_s[k1[0], h, k1[1]], qt) + bias_s[b1],
                    dot1(k_s[k2[0], h, k2[1]], qt) + bias_s[b2],
                )

            ahead = score(0)
            for a in group:
                s1, s2 = ahead
                if a + 1 < LANES:
                    ahead = score(a + 1)
                acc = value_term(a, prev[a])
                top = jnp.max(jnp.maximum(s1, s2), axis=0, keepdims=True) * SCALE
                m = jnp.maximum(m_old[a], top)
                alpha = jnp.exp2(m_old[a] - m)
                p1 = jnp.exp2(s1 * SCALE - m[:1])
                p2 = jnp.exp2(s2 * SCALE - m[:1])
                acc_s[prev[a][0]] = acc
                m_s[items[a][0]] = m
                l_s[items[a][0]] = l_old[a] * alpha + jnp.sum(p1 + p2, axis=0, keepdims=True)
                a_s[a] = alpha
                p_s[a] = jnp.concatenate([p1.astype(bf16), p2.astype(bf16)], axis=0)
            return carry

        def two_steps(t, carry, step=step):
            return step(2 * t + 1, step(2 * t, carry))

        turns = (list_ref[index, SLOTS - 1] + 1) // 2
        lax.fori_loop(0, turns, two_steps, 0)
        prev = codes(jnp.maximum(2 * turns - 1, 0))
        for a in group:
            acc_s[prev[a][0]] = value_term(a, prev[a])
    if last:
        sub = lax.broadcasted_iota(jnp.int32, (LSE, BLK), 0)
        for n in range(m_s.shape[0] - 1):
            total = l_s[n][:1]
            some = total > 0.0
            safe = jnp.where(some, total, 1.0)
            lse = jnp.where(some, m_s[n][:1] + jnp.log2(safe), LOW)
            out_ref[n // (HL * NB), n % (HL * NB), :DH] = (acc_s[n] * (1.0 / safe)).astype(bf16)
            one = lse.astype(bf16).astype(f32)
            two = (lse - one).astype(bf16).astype(f32)
            three = (lse - one) - two
            extra = jnp.where(sub == 0, one, jnp.where(sub == 1, two, jnp.where(sub == 2, three, 0.0)))
            out_ref[n // (HL * NB), n % (HL * NB), DH:] = extra.astype(bf16)


def weight_block(weight_ref, index):
    width = weight_ref.shape[1] // (2 * YN)
    return weight_ref[:, pl.ds(pl.multiple_of(index * width, width), width)]


def combine_kernel(where_ref, *refs):
    parts, weight_ref, out_ref, mixed_ref = refs[:XN], refs[XN], refs[XN + 1], refs[XN + 2]
    y, core = where_ref[2], where_ref[3]
    for i in range(NB):
        mixed = []
        for h in range(HL):
            n = h * NB + i
            rows = []
            for part in parts:
                extra = part[n, DH:].astype(f32)
                rows.append(extra[:1] + extra[1:2] + extra[2:3])
            top = jnp.maximum(jnp.maximum(rows[0], rows[1]), jnp.maximum(rows[2], rows[3]))
            shares = [jnp.exp2(r - top) for r in rows]
            scale = 1.0 / (shares[0] + shares[1] + shares[2] + shares[3])
            acc = parts[0][n, :DH].astype(f32) * (shares[0] * scale)
            for part, share in zip(parts[1:], shares[1:]):
                acc = acc + part[n, :DH].astype(f32) * (share * scale)
            mixed.append(acc.astype(bf16))
        mixed_ref[pl.ds(i * BLK, BLK), :] = jnp.concatenate(mixed, axis=0).T
    for k in range(YN):
        block = weight_block(weight_ref, ((y + k) % YN) * 2 + 1 - core)
        out_ref[k] = dot1(mixed_ref[...], block).astype(bf16)


def own_terms_kernel(where_ref, mixed_ref, weight_ref, out_ref):
    y, core = where_ref[2], where_ref[3]
    for k in range(YN):
        out_ref[k] = dot1(
            mixed_ref[...], weight_block(weight_ref, ((y + k) % YN) * 2 + core)
        )


def pair_sum_kernel(own_ref, other_ref, keep_ref, *send_refs):
    keep_ref[...] = own_ref[0] + other_ref[0].astype(f32)
    for k, send in enumerate(send_refs):
        send[...] = (own_ref[k + 1] + other_ref[k + 1].astype(f32)).astype(bf16)


def final_sum_kernel(keep_ref, one_ref, two_ref, three_ref, out_ref):
    total = keep_ref[...] + one_ref[...].astype(f32)
    out_ref[...] = (total + (two_ref[...].astype(f32) + three_ref[...].astype(f32))).astype(bf16)


def list_kernel(where_ref, mask_ref, out_ref):
    z, x = where_ref[0], where_ref[1]
    rows = [mask_ref[h, pl.ds(pl.multiple_of(z * XN * NB, XN * NB), XN * NB), :] for h in range(HL)]
    rows = jnp.where(jnp.concatenate(rows * len(CALLS), axis=0) == 1, 1.0, 0.0).astype(bf16)
    slots = XN * NB
    sub = lax.broadcasted_iota(jnp.int32, (slots, BLK), 0)
    lane = lax.broadcasted_iota(jnp.int32, (slots, BLK), 1)
    picked = jnp.zeros((slots, BLK), f32)
    kpos = jnp.full((slots, BLK), -1, jnp.int32)
    for c, js in enumerate(CALLS):
        target = jnp.full((slots, BLK), -1, jnp.int32)
        for r, j in enumerate(js):
            place = (((z - j + ZN) % ZN) * XN + x) * NB + (sub & 3)
            target = jnp.where((sub >> 2) == r, place, target)
        chosen = dot1(jnp.where(lane == target, 1.0, 0.0).astype(bf16), rows, NT)
        picked = jnp.where((lane >> 5) == c, chosen, picked)
        kpos = jnp.where((lane >> 5) == c, target, kpos)
    qpos = z * slots + (lane & 15)
    allowed = (picked > 0.5) & (kpos <= qpos)
    flag = jnp.where(allowed, 1.0, 0.0)
    row16 = lax.broadcasted_iota(jnp.int32, (slots, slots), 0)
    col16 = lax.broadcasted_iota(jnp.int32, (slots, slots), 1)
    earlier = dot1(jnp.where(col16 < row16, 1.0, 0.0).astype(bf16), flag.astype(bf16))
    earlier = jnp.where(allowed, earlier, -1.0)
    value = jnp.where(kpos == qpos, sub + 16, sub).astype(f32)
    total = jnp.sum(flag, axis=0, keepdims=True)
    one = lax.broadcasted_iota(jnp.int32, (1, BLK), 1)
    shift = (x - ((one >> 2) & 3) + XN) % XN
    query = shift * (HL * NB) + ((one >> 4) & 1) * NB + (one & 3)
    ranks = 3 * NB // 2

    def nth(p):
        at = jnp.sum(jnp.where(earlier == float(p), value, 0.0), axis=0, keepdims=True)
        return jnp.where(total > float(p), at, 32.0).astype(jnp.int32)

    pairs = []
    for p in range(ranks):
        first, second = nth(2 * p), nth(2 * p + 1)
        code = ((first & 15) << 6) + ((second & 15) << 10)
        pairs.append(code + ((first >> 4) << 14) + ((second >> 4) << 16))
    sub8 = lax.broadcasted_iota(jnp.int32, (8, BLK), 0)
    ra = lax.broadcasted_iota(jnp.int32, (BLK, BLK), 0)
    ca = lax.broadcasted_iota(jnp.int32, (BLK, BLK), 1)
    same = (ra >> 5) == (ca >> 5)
    below = jnp.where(same & (ra < ca), 1.0, 0.0).astype(bf16)
    within = jnp.where(same, 1.0, 0.0).astype(bf16)
    ident = jnp.where(ra == ca, 1.0, 0.0).astype(bf16)
    spot = lax.broadcasted_iota(jnp.int32, (BLK, SLOTS), 1).astype(f32)
    third = sub // 3
    piece = sub - third * 3
    end = lax.broadcasted_iota(jnp.int32, (1, SLOTS), 1)
    for own in range(2):
        mine = (shift == 0) if own else (shift > 0)
        offset, dummy = (0, HL * NB) if own else (HL * NB, AWAY)
        dummy = dummy + (2 << 14) + (2 << 16)
        valid = jnp.zeros((8, BLK), f32)
        for p in range(ranks):
            valid = jnp.where((sub8 == p) & (total > float(2 * p)) & mine, 1.0, valid)
        valid16 = valid.astype(bf16)
        rank = dot1(valid16, below)
        used = (dot1(valid16, within).astype(jnp.int32) + (LANES - 1)) // LANES
        base = jnp.zeros((1, BLK), jnp.int32)
        place = jnp.full((8, BLK), -1.0, f32)
        for p in range(ranks):
            at = base.astype(f32) * float(LANES) + rank
            place = jnp.where((sub8 == p) & (valid > 0.5), at, place)
            base = base + used[p : p + 1]
        column = dot1(ident, place.astype(bf16), NT)
        acc = jnp.zeros((slots, SLOTS), f32)
        for p in range(ranks):
            code = pairs[p] + (query - offset)
            part = jnp.where(
                piece == 0, code & 255, jnp.where(piece == 1, (code >> 8) & 255, code >> 16)
            )
            part = jnp.where((lane >> 5) == third, part.astype(f32), 0.0)
            part = jnp.where(sub < 12, part, jnp.where((lane >> 5) == sub - 12, 1.0, 0.0))
            hit = jnp.where(column[:, p : p + 1] == spot, 1.0, 0.0).astype(bf16)
            acc = acc + dot1(part.astype(bf16), hit)
        for c in range(len(CALLS)):
            low, mid, high = [acc[3 * c + k : 3 * c + k + 1].astype(jnp.int32) for k in range(3)]
            items = low + (mid << 8) + (high << 16)
            items = jnp.where(acc[12 + c : 13 + c] > 0.5, items, dummy)
            count = jnp.max(jnp.where((one >> 5) == c, base, 0), axis=1, keepdims=True)
            out_ref[4 * own + c : 4 * own + c + 1, :] = jnp.where(end == SLOTS - 1, count, items)


def call(kernel, outs, ins, scratch=(), smem=0, flops=1e9, mib=16):
    size = sum(math.prod(a.shape) * a.dtype.itemsize for a in ins)
    return pl.pallas_call(
        kernel,
        out_shape=outs,
        in_specs=[SMEM] * smem + [VMEM] * (len(ins) - smem),
        out_specs=jax.tree.map(lambda _: VMEM, outs),
        scratch_shapes=list(scratch),
        compiler_params=params(mib),
        cost_estimate=pl.CostEstimate(flops=int(flops), bytes_accessed=size, transcendentals=0),
    )(*ins)


def shape(*dims, dtype=f32):
    return jax.ShapeDtypeStruct(dims, dtype)


def along_z(value, step):
    pairs = [(z * XN + x, ((z + step) % ZN) * XN + x) for z in range(ZN) for x in range(XN)]
    return lax.ppermute(value, "seq", pairs)


def up_z(value, step):
    pairs = [(z * XN + x, (z + step) * XN + x) for z in range(ZN - step) for x in range(XN)]
    return lax.ppermute(value, "seq", pairs)


def along_x(value, step):
    pairs = [(z * XN + x, z * XN + (x + step) % XN) for z in range(ZN) for x in range(XN)]
    return lax.ppermute(value, "seq", pairs)


def sibling(value):
    return lax.ppermute(value, "head", [(g, g ^ 1) for g in range(2 * YN)])


def along_y(value, step):
    pairs = [(g, (g + 2 * step) % (2 * YN)) for g in range(2 * YN)]
    return lax.ppermute(value, "head", pairs)


def on_device(query, key, value, reflect, block_mask, out_weight):
    here, group = lax.axis_index("seq"), lax.axis_index("head")
    z, x = here // XN, here % XN
    where = jnp.stack([z, x, group // 2, group % 2]).astype(jnp.int32)
    width = out_weight.shape[1] // (2 * YN)
    tokens = query.shape[0]
    tie = lambda *values: lax.optimization_barrier(values)
    square = shape(HL, DH, DH)
    blocks = shape(HL, NB, BLK, DH)
    keys16 = shape(HL, NB, BLK, DH, dtype=bf16)
    v_rows = [None] * ZN
    reflect_h = reflect.transpose(1, 0, 2)
    tri, frames, total = call(
        factor_kernel, (blocks, shape(HL, NB - 1, DH, DH), square), (reflect_h,), flops=2e9
    )
    block_mask, value, total = tie(block_mask, value, total)
    v_rows[0] = value.reshape(NB, BLK, HL, DH).transpose(2, 0, 3, 1)
    others = [along_x(total, k) for k in range(1, XN)]
    v_rows[1], v_rows[7] = along_z(v_rows[0], 1), along_z(v_rows[0], -1)
    lists = call(list_kernel, shape(8, SLOTS, dtype=jnp.int32), (where, block_mask), smem=1)
    *others, lists = tie(*others, lists)
    before, total = call(
        row_kernel, (square, square), (where, total, *others), smem=1
    )
    total, query, key = tie(total, query, key)
    left = up_z(total, 1)
    _, v_rows[7] = tie(total, v_rows[7])
    v_rows[6] = along_z(v_rows[7], -1)
    q_local, k_local = call(
        local_kernel,
        (blocks, blocks),
        (query.transpose(1, 0, 2), key.transpose(1, 0, 2), reflect_h, tri, frames),
        flops=2e9,
    )
    left, q_local, k_local, v_rows[1] = tie(left, q_local, k_local, v_rows[1])
    total, chain = call(partial(hop_kernel, 1), (square, square), (where, left, total), smem=1)
    left = up_z(total, 2)
    _, v_rows[6] = tie(total, v_rows[6])
    v_rows[5] = along_z(v_rows[6], -1)
    total, chain = call(
        partial(hop_kernel, 2), (square, square), (where, left, total, chain), smem=1
    )
    left = up_z(total, 4)
    _, v_rows[5] = tie(total, v_rows[5])
    v_rows[4] = along_z(v_rows[5], -1)
    k_turned, q_turned = call(
        turn_kernel, (keys16, keys16), (where, left, chain, before, q_local, k_local), smem=1
    )
    k_rows = [k_turned, along_z(k_turned, 1)] + [None] * 5 + [along_z(k_turned, -1)]
    lanes = [along_x(q_turned, k) for k in range(1, XN)]
    _, v_rows[1] = tie(k_turned, v_rows[1])
    v_rows[2] = along_z(v_rows[1], 1)

    def blank(slots):
        return (shape(slots + 1, 8, BLK), shape(slots + 1, 8, BLK), shape(slots + 1, DH, BLK))

    def attend(work, js, carried, slots, first, last):
        queries = lanes if slots == AWAY else [q_turned]
        outs = shape(slots // (HL * NB), HL * NB, DH + LSE, BLK, dtype=bf16) if last else blank(slots)
        scratch = [pltpu.VMEM(a.shape, f32) for a in blank(slots)] if last else []
        scratch += [pltpu.VMEM((slots + 1, DH, BLK), bf16)]
        scratch += [pltpu.VMEM((len(js), HL, NB, BLK, DH), bf16)] * 2
        scratch += [pltpu.VMEM((3, BLK, BLK), f32), pltpu.VMEM((LANES, 2 * BLK, BLK), bf16)]
        scratch += [pltpu.VMEM((LANES, 8, BLK), f32)]
        return call(
            partial(attend_kernel, work, len(queries), first, last, len(js)),
            outs,
            (lists, *queries, *[k_rows[j] for j in js], *[v_rows[j] for j in js], *carried),
            scratch=scratch,
            smem=1,
            flops=2e9 * len(js),
            mib=16,
        )

    k_rows[1], k_rows[7], v_rows[4] = tie(k_rows[1], k_rows[7], v_rows[4])
    v_rows[3] = along_z(v_rows[4], -1)
    k_rows[2], k_rows[6] = along_z(k_rows[1], 1), along_z(k_rows[7], -1)
    state = attend(((0, 0),), CALLS[0], (), AWAY, True, False)
    state, k_rows[2], k_rows[6] = tie(state, k_rows[2], k_rows[6])
    k_rows[3], k_rows[5] = along_z(k_rows[2], 1), along_z(k_rows[6], -1)
    state = attend(((1, 0),), CALLS[1], state, AWAY, False, False)
    state, k_rows[3], k_rows[5] = tie(state, k_rows[3], k_rows[5])
    k_rows[4] = along_z(k_rows[3], 1)
    state = attend(((2, 0),), CALLS[2], state, AWAY, False, False)
    away = attend(((3, 0),), CALLS[3], state, AWAY, False, True)
    got = [along_x(away[a - 1], -a) for a in range(1, XN)]
    away, q_turned = tie(away, q_turned)
    work = ((4, 0), (5, 3), (6, 5), (7, 7))
    mine = attend(work, sum(CALLS, ()), (), HL * NB, True, True)
    got = [mine[0]] + got
    sends, mixed = call(
        combine_kernel,
        (shape(YN, tokens, width, dtype=bf16), shape(tokens, HL * DH, dtype=bf16)),
        (where, *got, out_weight),
        smem=1,
    )
    other = sibling(sends)
    own = call(own_terms_kernel, shape(YN, tokens, width), (where, mixed, out_weight), smem=1)
    part = shape(tokens, width, dtype=bf16)
    keep, *sends = call(
        pair_sum_kernel, (shape(tokens, width), part, part, part), (own, other)
    )
    got = [along_y(sends[k - 1], k) for k in range(1, YN)]
    return call(final_sum_kernel, part, (keep, *got))


def solution(mesh):
    in_specs = (
        P("seq", "head", None),
        P("seq", "head", None),
        P("seq", "head", None),
        P("seq", "head", None),
        P("head", None, None),
        P("head", None),
    )
    out_specs = P("seq", "head")
    return jax.shard_map(
        on_device, mesh=mesh, in_specs=in_specs, out_specs=out_specs, check_vma=False
    )
```

```python
from functools import partial
import math

import jax
import jax.numpy as jnp
from jax import lax
from jax.experimental import pallas as pl
from jax.experimental.pallas import tpu as pltpu
from jax.sharding import PartitionSpec as P

BLK = 128
DH = 128
XN = 4
ZN = 8
HL = 2
NB = 4
YN = 4
QB = HL * XN * NB
LANES = 8
AWAY = QB - HL * NB
LSE = 16
SLOTS = 256
CALLS = ((0, 1, 7), (2, 6), (3, 5), (4,))
EPSILON = 1e-06
LOW = -1e30
SCALE = math.log2(math.e) / math.sqrt(DH)
f32 = jnp.float32
bf16 = jnp.bfloat16
NN = ((1,), (0,))
NT = ((1,), (1,))
TN = ((0,), (0,))
VMEM = pl.BlockSpec(memory_space=pltpu.VMEM)
SMEM = pl.BlockSpec(memory_space=pltpu.SMEM)


def params(mib):
    return pltpu.CompilerParams(vmem_limit_bytes=mib * 1024 * 1024)


def dot1(a, b, dims=NN):
    return lax.dot_general(a, b, (dims, ((), ())), preferred_element_type=f32)


def halves(a):
    high = a.astype(bf16)
    return high, (a - high.astype(f32)).astype(bf16)


def dot3(a, b, dims=NN):
    ah, al = halves(a)
    bh, bl = halves(b)
    ca, cb = dims[0][0], dims[1][0]
    both = dot1(jnp.concatenate([ah, al], axis=ca), jnp.concatenate([bh, bh], axis=cb), dims)
    return both + dot1(ah, bl, dims)


def eye():
    row = lax.broadcasted_iota(jnp.int32, (BLK, BLK), 0)
    col = lax.broadcasted_iota(jnp.int32, (BLK, BLK), 1)
    return jnp.where(row == col, 1.0, 0.0).astype(f32)


def unit_rows(values):
    values = values.astype(f32)
    return values * lax.rsqrt(jnp.sum(values * values, axis=-1, keepdims=True) + EPSILON)


def factor_kernel(reflect_ref, tri_ref, frames_ref, total_ref):
    row = lax.broadcasted_iota(jnp.int32, (BLK, BLK), 0)
    col = lax.broadcasted_iota(jnp.int32, (BLK, BLK), 1)
    ident = jnp.where(row == col, 1.0, 0.0).astype(f32)
    items = [(h, b) for h in range(HL) for b in range(NB)]
    units = [unit_rows(reflect_ref[h, pl.ds(b * BLK, BLK), :]) for h, b in items]
    grams = [2.0 * dot3(u, u, NT) for u in units]
    inv = [ident - jnp.where((row // 2 == col // 2) & (row < col), g, 0.0) for g in grams]
    size = 2
    while size < BLK:
        off = (row // (2 * size) == col // (2 * size)) & (row // size < col // size)
        mids = [dot3(x, jnp.where(off, g, 0.0)) for x, g in zip(inv, grams)]
        inv = [x - dot3(m, x) for x, m in zip(inv, mids)]
        size *= 2
    wholes = []
    for (h, b), u, x in zip(items, units, inv):
        tri = 2.0 * x
        tri_ref[h, b] = tri
        wholes.append(ident - dot3(u, dot3(tri, u), TN))
    frames = [wholes[h * NB] for h in range(HL)]
    for b in range(1, NB):
        for h in range(HL):
            frames_ref[h, b - 1] = frames[h]
        frames = [dot3(frames[h], wholes[h * NB + b]) for h in range(HL)]
    for h in range(HL):
        total_ref[h] = frames[h]


def local_kernel(query_ref, key_ref, reflect_ref, tri_ref, frames_ref, qt_ref, k_ref):
    row = lax.broadcasted_iota(jnp.int32, (2 * BLK, BLK), 0) % BLK
    col = lax.broadcasted_iota(jnp.int32, (2 * BLK, BLK), 1)
    lower = col <= row
    for h in range(HL):
        for b in range(NB):
            here = pl.ds(b * BLK, BLK)
            unit = unit_rows(reflect_ref[h, here, :])
            uh, ul = halves(unit)
            both = jnp.concatenate([query_ref[h, here, :], key_ref[h, here, :]], axis=0)
            twice = jnp.concatenate([both, both], axis=1)
            proj = dot1(twice, jnp.concatenate([uh, ul], axis=1), NT)
            coef = dot3(jnp.where(lower, proj, 0.0), tri_ref[h, b], NT)
            turned = both.astype(f32) - dot3(coef, unit)
            if b > 0:
                turned = dot3(turned, frames_ref[h, b - 1], NT)
            qt_ref[h, b] = turned[:BLK].T
            k_ref[h, b] = turned[BLK:]


def row_kernel(where_ref, own_ref, one_ref, two_ref, three_ref, before_ref, total_ref):
    x = where_ref[1]
    for h in range(HL):
        cands = [own_ref[h], one_ref[h], two_ref[h], three_ref[h]]

        def pick(i):
            out = cands[0]
            for k in range(1, XN):
                out = jnp.where((x - k + XN) % XN == i, cands[k], out)
            return out

        first = pick(0)
        second = dot3(first, pick(1))
        third = dot3(second, pick(2))
        before = jnp.where(x == 0, eye(), first)
        before = jnp.where(x == 2, second, before)
        before_ref[h] = jnp.where(x == 3, third, before)
        total_ref[h] = dot3(third, pick(3))


def hop_kernel(step, where_ref, left_ref, total_ref, *refs):
    z = where_ref[0]
    total_out, chain_out = refs[-2:]
    for h in range(HL):
        left = jnp.where(z >= step, left_ref[h], eye())
        total_out[h] = dot3(left, total_ref[h])
        chain_out[h] = left if step == 1 else dot3(left, refs[0][h])


def turn_kernel(where_ref, left_ref, chain_ref, before_ref, qt_ref, k_ref, k_out, qt_out):
    z = where_ref[0]
    for h in range(HL):
        left = jnp.where(z >= 4, left_ref[h], eye())
        frame = dot3(left, dot3(chain_ref[h], before_ref[h]))
        for b in range(NB):
            k_out[h, b] = dot3(k_ref[h, b], frame, NT).astype(bf16)
            qt_out[h, b] = dot3(frame, qt_ref[h, b]).astype(bf16)


def attend_kernel(work, lanes, first, last, rows, *refs):
    refs = list(refs)
    list_ref, queries, refs = refs[0], refs[1 : 1 + lanes], refs[1 + lanes :]
    keys, values = refs[:rows], refs[rows : 2 * rows]
    refs = refs[2 * rows :]
    carried = None
    if not first:
        carried, refs = refs[:3], refs[3:]
    if last:
        out_ref, m_s, l_s, acc_s, q_s, k_s, v_s, bias_s, p_s, a_s = refs
    else:
        m_s, l_s, acc_s, q_s, k_s, v_s, bias_s, p_s, a_s = refs
    for r in range(rows):
        k_s[r] = keys[r][...]
        v_s[r] = values[r][...]
    for a in range(lanes):
        for h in range(HL):
            for i in range(NB):
                q_s[(a * HL + h) * NB + i] = queries[a][h, i]
    q_s[lanes * HL * NB] = jnp.zeros((DH, BLK), bf16)
    krow = lax.broadcasted_iota(jnp.int32, (BLK, BLK), 0)
    qcol = lax.broadcasted_iota(jnp.int32, (BLK, BLK), 1)
    bias_s[0] = jnp.zeros((BLK, BLK), f32)
    bias_s[1] = jnp.where(krow <= qcol, 0.0, LOW).astype(f32)
    bias_s[2] = jnp.full((BLK, BLK), LOW, f32)
    if first:
        m_s[...] = jnp.full(m_s.shape, LOW, f32)
        l_s[...] = jnp.zeros(l_s.shape, f32)
        acc_s[...] = jnp.zeros(acc_s.shape, f32)
    else:
        m_s[...] = carried[0][...]
        l_s[...] = carried[1][...]
        acc_s[...] = carried[2][...]
    group = range(LANES)

    for index, base in work:
        p_s[...] = jnp.zeros(p_s.shape, bf16)
        a_s[...] = jnp.ones(a_s.shape, f32)

        def codes(t, index=index, base=base):
            out = []
            for a in group:
                code = list_ref[index, t * LANES + a]
                out.append(
                    (
                        code & 63,
                        (code >> 2) & 1,
                        (((code >> 8) & 3) + base, (code >> 6) & 3),
                        (((code >> 12) & 3) + base, (code >> 10) & 3),
                        (code >> 14) & 3,
                        (code >> 16) & 3,
                    )
                )
            return out

        def value_term(a, item):
            qi, h, k1, k2 = item[:4]
            vt = jnp.concatenate([v_s[k1[0], h, k1[1]], v_s[k2[0], h, k2[1]]], axis=1)
            return acc_s[qi] * a_s[a][:1] + dot1(vt, p_s[a])

        def step(t, carry, codes=codes, value_term=value_term):
            prev = codes(jnp.maximum(t - 1, 0))
            items = codes(t)
            m_old = [m_s[c[0]] for c in items]
            l_old = [l_s[c[0]] for c in items]

            def score(a):
                qi, h, k1, k2, b1, b2 = items[a]
                qt = q_s[qi]
                return (
                    dot1(k_s[k1[0], h, k1[1]], qt) + bias_s[b1],
                    dot1(k_s[k2[0], h, k2[1]], qt) + bias_s[b2],
                )

            ahead = score(0)
            for a in group:
                s1, s2 = ahead
                if a + 1 < LANES:
                    ahead = score(a + 1)
                acc = value_term(a, prev[a])
                top = jnp.max(jnp.maximum(s1, s2), axis=0, keepdims=True) * SCALE
                m = jnp.maximum(m_old[a], top)
                alpha = jnp.exp2(m_old[a] - m)
                p1 = jnp.exp2(s1 * SCALE - m[:1])
                p2 = jnp.exp2(s2 * SCALE - m[:1])
                acc_s[prev[a][0]] = acc
                m_s[items[a][0]] = m
                l_s[items[a][0]] = l_old[a] * alpha + jnp.sum(p1 + p2, axis=0, keepdims=True)
                a_s[a] = alpha
                p_s[a] = jnp.concatenate([p1.astype(bf16), p2.astype(bf16)], axis=0)
            return carry

        def two_steps(t, carry, step=step):
            return step(2 * t + 1, step(2 * t, carry))

        turns = (list_ref[index, SLOTS - 1] + 1) // 2
        lax.fori_loop(0, turns, two_steps, 0)
        prev = codes(jnp.maximum(2 * turns - 1, 0))
        for a in group:
            acc_s[prev[a][0]] = value_term(a, prev[a])
    if last:
        sub = lax.broadcasted_iota(jnp.int32, (LSE, BLK), 0)
        for n in range(m_s.shape[0] - 1):
            total = l_s[n][:1]
            some = total > 0.0
            safe = jnp.where(some, total, 1.0)
            lse = jnp.where(some, m_s[n][:1] + jnp.log2(safe), LOW)
            out_ref[n // (HL * NB), n % (HL * NB), :DH] = (acc_s[n] * (1.0 / safe)).astype(bf16)
            one = lse.astype(bf16).astype(f32)
            two = (lse - one).astype(bf16).astype(f32)
            three = (lse - one) - two
            extra = jnp.where(sub == 0, one, jnp.where(sub == 1, two, jnp.where(sub == 2, three, 0.0)))
            out_ref[n // (HL * NB), n % (HL * NB), DH:] = extra.astype(bf16)


def weight_block(weight_ref, index):
    width = weight_ref.shape[1] // (2 * YN)
    return weight_ref[:, pl.ds(pl.multiple_of(index * width, width), width)]


def combine_kernel(where_ref, *refs):
    parts, weight_ref, out_ref, mixed_ref = refs[:XN], refs[XN], refs[XN + 1], refs[XN + 2]
    y, core = where_ref[2], where_ref[3]
    for i in range(NB):
        mixed = []
        for h in range(HL):
            n = h * NB + i
            rows = []
            for part in parts:
                extra = part[n, DH:].astype(f32)
                rows.append(extra[:1] + extra[1:2] + extra[2:3])
            top = jnp.maximum(jnp.maximum(rows[0], rows[1]), jnp.maximum(rows[2], rows[3]))
            shares = [jnp.exp2(r - top) for r in rows]
            scale = 1.0 / (shares[0] + shares[1] + shares[2] + shares[3])
            acc = parts[0][n, :DH].astype(f32) * (shares[0] * scale)
            for part, share in zip(parts[1:], shares[1:]):
                acc = acc + part[n, :DH].astype(f32) * (share * scale)
            mixed.append(acc.astype(bf16))
        mixed_ref[pl.ds(i * BLK, BLK), :] = jnp.concatenate(mixed, axis=0).T
    for k in range(YN):
        block = weight_block(weight_ref, ((y + k) % YN) * 2 + 1 - core)
        out_ref[k] = dot1(mixed_ref[...], block).astype(bf16)


def own_terms_kernel(where_ref, mixed_ref, weight_ref, out_ref):
    y, core = where_ref[2], where_ref[3]
    for k in range(YN):
        out_ref[k] = dot1(
            mixed_ref[...], weight_block(weight_ref, ((y + k) % YN) * 2 + core)
        )


def pair_sum_kernel(own_ref, other_ref, keep_ref, *send_refs):
    keep_ref[...] = own_ref[0] + other_ref[0].astype(f32)
    for k, send in enumerate(send_refs):
        send[...] = (own_ref[k + 1] + other_ref[k + 1].astype(f32)).astype(bf16)


def final_sum_kernel(keep_ref, one_ref, two_ref, three_ref, out_ref):
    total = keep_ref[...] + one_ref[...].astype(f32)
    out_ref[...] = (total + (two_ref[...].astype(f32) + three_ref[...].astype(f32))).astype(bf16)


def list_kernel(where_ref, mask_ref, out_ref):
    z, x = where_ref[0], where_ref[1]
    rows = [mask_ref[h, pl.ds(pl.multiple_of(z * XN * NB, XN * NB), XN * NB), :] for h in range(HL)]
    rows = jnp.where(jnp.concatenate(rows * len(CALLS), axis=0) == 1, 1.0, 0.0).astype(bf16)
    slots = XN * NB
    sub = lax.broadcasted_iota(jnp.int32, (slots, BLK), 0)
    lane = lax.broadcasted_iota(jnp.int32, (slots, BLK), 1)
    picked = jnp.zeros((slots, BLK), f32)
    kpos = jnp.full((slots, BLK), -1, jnp.int32)
    for c, js in enumerate(CALLS):
        target = jnp.full((slots, BLK), -1, jnp.int32)
        for r, j in enumerate(js):
            place = (((z - j + ZN) % ZN) * XN + x) * NB + (sub & 3)
            target = jnp.where((sub >> 2) == r, place, target)
        chosen = dot1(jnp.where(lane == target, 1.0, 0.0).astype(bf16), rows, NT)
        picked = jnp.where((lane >> 5) == c, chosen, picked)
        kpos = jnp.where((lane >> 5) == c, target, kpos)
    qpos = z * slots + (lane & 15)
    allowed = (picked > 0.5) & (kpos <= qpos)
    flag = jnp.where(allowed, 1.0, 0.0)
    row16 = lax.broadcasted_iota(jnp.int32, (slots, slots), 0)
    col16 = lax.broadcasted_iota(jnp.int32, (slots, slots), 1)
    earlier = dot1(jnp.where(col16 < row16, 1.0, 0.0).astype(bf16), flag.astype(bf16))
    earlier = jnp.where(allowed, earlier, -1.0)
    value = jnp.where(kpos == qpos, sub + 16, sub).astype(f32)
    total = jnp.sum(flag, axis=0, keepdims=True)
    one = lax.broadcasted_iota(jnp.int32, (1, BLK), 1)
    shift = (x - ((one >> 2) & 3) + XN) % XN
    query = shift * (HL * NB) + ((one >> 4) & 1) * NB + (one & 3)
    ranks = 3 * NB // 2

    def nth(p):
        at = jnp.sum(jnp.where(earlier == float(p), value, 0.0), axis=0, keepdims=True)
        return jnp.where(total > float(p), at, 32.0).astype(jnp.int32)

    pairs = []
    for p in range(ranks):
        first, second = nth(2 * p), nth(2 * p + 1)
        code = ((first & 15) << 6) + ((second & 15) << 10)
        pairs.append(code + ((first >> 4) << 14) + ((second >> 4) << 16))
    sub8 = lax.broadcasted_iota(jnp.int32, (8, BLK), 0)
    ra = lax.broadcasted_iota(jnp.int32, (BLK, BLK), 0)
    ca = lax.broadcasted_iota(jnp.int32, (BLK, BLK), 1)
    same = (ra >> 5) == (ca >> 5)
    below = jnp.where(same & (ra < ca), 1.0, 0.0).astype(bf16)
    within = jnp.where(same, 1.0, 0.0).astype(bf16)
    ident = jnp.where(ra == ca, 1.0, 0.0).astype(bf16)
    spot = lax.broadcasted_iota(jnp.int32, (BLK, SLOTS), 1).astype(f32)
    third = sub // 3
    piece = sub - third * 3
    end = lax.broadcasted_iota(jnp.int32, (1, SLOTS), 1)
    for own in range(2):
        mine = (shift == 0) if own else (shift > 0)
        offset, dummy = (0, HL * NB) if own else (HL * NB, AWAY)
        dummy = dummy + (2 << 14) + (2 << 16)
        valid = jnp.zeros((8, BLK), f32)
        for p in range(ranks):
            valid = jnp.where((sub8 == p) & (total > float(2 * p)) & mine, 1.0, valid)
        valid16 = valid.astype(bf16)
        rank = dot1(valid16, below)
        used = (dot1(valid16, within).astype(jnp.int32) + (LANES - 1)) // LANES
        base = jnp.zeros((1, BLK), jnp.int32)
        place = jnp.full((8, BLK), -1.0, f32)
        for p in range(ranks):
            at = base.astype(f32) * float(LANES) + rank
            place = jnp.where((sub8 == p) & (valid > 0.5), at, place)
            base = base + used[p : p + 1]
        column = dot1(ident, place.astype(bf16), NT)
        acc = jnp.zeros((slots, SLOTS), f32)
        for p in range(ranks):
            code = pairs[p] + (query - offset)
            part = jnp.where(
                piece == 0, code & 255, jnp.where(piece == 1, (code >> 8) & 255, code >> 16)
            )
            part = jnp.where((lane >> 5) == third, part.astype(f32), 0.0)
            part = jnp.where(sub < 12, part, jnp.where((lane >> 5) == sub - 12, 1.0, 0.0))
            hit = jnp.where(column[:, p : p + 1] == spot, 1.0, 0.0).astype(bf16)
            acc = acc + dot1(part.astype(bf16), hit)
        for c in range(len(CALLS)):
            low, mid, high = [acc[3 * c + k : 3 * c + k + 1].astype(jnp.int32) for k in range(3)]
            items = low + (mid << 8) + (high << 16)
            items = jnp.where(acc[12 + c : 13 + c] > 0.5, items, dummy)
            count = jnp.max(jnp.where((one >> 5) == c, base, 0), axis=1, keepdims=True)
            out_ref[4 * own + c : 4 * own + c + 1, :] = jnp.where(end == SLOTS - 1, count, items)


def call(kernel, outs, ins, scratch=(), smem=0, flops=1e9, mib=16):
    size = sum(math.prod(a.shape) * a.dtype.itemsize for a in ins)
    return pl.pallas_call(
        kernel,
        out_shape=outs,
        in_specs=[SMEM] * smem + [VMEM] * (len(ins) - smem),
        out_specs=jax.tree.map(lambda _: VMEM, outs),
        scratch_shapes=list(scratch),
        compiler_params=params(mib),
        cost_estimate=pl.CostEstimate(flops=int(flops), bytes_accessed=size, transcendentals=0),
    )(*ins)


def shape(*dims, dtype=f32):
    return jax.ShapeDtypeStruct(dims, dtype)


def along_z(value, step):
    pairs = [(z * XN + x, ((z + step) % ZN) * XN + x) for z in range(ZN) for x in range(XN)]
    return lax.ppermute(value, "seq", pairs)


def up_z(value, step):
    pairs = [(z * XN + x, (z + step) * XN + x) for z in range(ZN - step) for x in range(XN)]
    return lax.ppermute(value, "seq", pairs)


def along_x(value, step):
    pairs = [(z * XN + x, z * XN + (x + step) % XN) for z in range(ZN) for x in range(XN)]
    return lax.ppermute(value, "seq", pairs)


def sibling(value):
    return lax.ppermute(value, "head", [(g, g ^ 1) for g in range(2 * YN)])


def along_y(value, step):
    pairs = [(g, (g + 2 * step) % (2 * YN)) for g in range(2 * YN)]
    return lax.ppermute(value, "head", pairs)


def on_device(query, key, value, reflect, block_mask, out_weight):
    here, group = lax.axis_index("seq"), lax.axis_index("head")
    z, x = here // XN, here % XN
    where = jnp.stack([z, x, group // 2, group % 2]).astype(jnp.int32)
    width = out_weight.shape[1] // (2 * YN)
    tokens = query.shape[0]
    tie = lambda *values: lax.optimization_barrier(values)
    square = shape(HL, DH, DH)
    blocks = shape(HL, NB, BLK, DH)
    keys16 = shape(HL, NB, BLK, DH, dtype=bf16)
    v_rows = [None] * ZN
    reflect_h = reflect.transpose(1, 0, 2)
    tri, frames, total = call(
        factor_kernel, (blocks, shape(HL, NB - 1, DH, DH), square), (reflect_h,), flops=2e9
    )
    block_mask, value, total = tie(block_mask, value, total)
    v_rows[0] = value.reshape(NB, BLK, HL, DH).transpose(2, 0, 3, 1)
    others = [along_x(total, k) for k in range(1, XN)]
    v_rows[1], v_rows[7] = along_z(v_rows[0], 1), along_z(v_rows[0], -1)
    lists = call(list_kernel, shape(8, SLOTS, dtype=jnp.int32), (where, block_mask), smem=1)
    *others, lists = tie(*others, lists)
    before, total = call(
        row_kernel, (square, square), (where, total, *others), smem=1
    )
    total, query, key = tie(total, query, key)
    left = up_z(total, 1)
    _, v_rows[1], v_rows[7] = tie(total, v_rows[1], v_rows[7])
    v_rows[2], v_rows[6] = along_z(v_rows[1], 1), along_z(v_rows[7], -1)
    q_local, k_local = call(
        local_kernel,
        (blocks, blocks),
        (query.transpose(1, 0, 2), key.transpose(1, 0, 2), reflect_h, tri, frames),
        flops=2e9,
    )
    left, q_local, k_local = tie(left, q_local, k_local)
    total, chain = call(partial(hop_kernel, 1), (square, square), (where, left, total), smem=1)
    left = up_z(total, 2)
    _, v_rows[6] = tie(total, v_rows[6])
    v_rows[5] = along_z(v_rows[6], -1)
    total, chain = call(
        partial(hop_kernel, 2), (square, square), (where, left, total, chain), smem=1
    )
    left = up_z(total, 4)
    _, v_rows[5] = tie(total, v_rows[5])
    v_rows[4] = along_z(v_rows[5], -1)
    k_turned, q_turned = call(
        turn_kernel, (keys16, keys16), (where, left, chain, before, q_local, k_local), smem=1
    )
    k_rows = [k_turned, along_z(k_turned, 1)] + [None] * 5 + [along_z(k_turned, -1)]
    lanes = [along_x(q_turned, k) for k in range(1, XN)]

    def blank(slots):
        return (shape(slots + 1, 8, BLK), shape(slots + 1, 8, BLK), shape(slots + 1, DH, BLK))

    def attend(work, js, carried, slots, first, last):
        queries = lanes if slots == AWAY else [q_turned]
        outs = shape(slots // (HL * NB), HL * NB, DH + LSE, BLK, dtype=bf16) if last else blank(slots)
        scratch = [pltpu.VMEM(a.shape, f32) for a in blank(slots)] if last else []
        scratch += [pltpu.VMEM((slots + 1, DH, BLK), bf16)]
        scratch += [pltpu.VMEM((len(js), HL, NB, BLK, DH), bf16)] * 2
        scratch += [pltpu.VMEM((3, BLK, BLK), f32), pltpu.VMEM((LANES, 2 * BLK, BLK), bf16)]
        scratch += [pltpu.VMEM((LANES, 8, BLK), f32)]
        return call(
            partial(attend_kernel, work, len(queries), first, last, len(js)),
            outs,
            (lists, *queries, *[k_rows[j] for j in js], *[v_rows[j] for j in js], *carried),
            scratch=scratch,
            smem=1,
            flops=2e9 * len(js),
            mib=16,
        )

    k_rows[1], k_rows[7], v_rows[4] = tie(k_rows[1], k_rows[7], v_rows[4])
    v_rows[3] = along_z(v_rows[4], -1)
    k_rows[2], k_rows[6] = along_z(k_rows[1], 1), along_z(k_rows[7], -1)
    state = attend(((0, 0),), CALLS[0], (), AWAY, True, False)
    state, k_rows[2], k_rows[6] = tie(state, k_rows[2], k_rows[6])
    k_rows[3], k_rows[5] = along_z(k_rows[2], 1), along_z(k_rows[6], -1)
    state = attend(((1, 0),), CALLS[1], state, AWAY, False, False)
    state, k_rows[3], k_rows[5] = tie(state, k_rows[3], k_rows[5])
    k_rows[4] = along_z(k_rows[3], 1)
    state = attend(((2, 0),), CALLS[2], state, AWAY, False, False)
    away = attend(((3, 0),), CALLS[3], state, AWAY, False, True)
    got = [along_x(away[a - 1], -a) for a in range(1, XN)]
    away, q_turned = tie(away, q_turned)
    work = ((4, 0), (5, 3), (6, 5), (7, 7))
    mine = attend(work, sum(CALLS, ()), (), HL * NB, True, True)
    got = [mine[0]] + got
    sends, mixed = call(
        combine_kernel,
        (shape(YN, tokens, width, dtype=bf16), shape(tokens, HL * DH, dtype=bf16)),
        (where, *got, out_weight),
        smem=1,
    )
    other = sibling(sends)
    own = call(own_terms_kernel, shape(YN, tokens, width), (where, mixed, out_weight), smem=1)
    part = shape(tokens, width, dtype=bf16)
    keep, *sends = call(
        pair_sum_kernel, (shape(tokens, width), part, part, part), (own, other)
    )
    got = [along_y(sends[k - 1], k) for k in range(1, YN)]
    return call(final_sum_kernel, part, (keep, *got))


def solution(mesh):
    in_specs = (
        P("seq", "head", None),
        P("seq", "head", None),
        P("seq", "head", None),
        P("seq", "head", None),
        P("head", None, None),
        P("head", None),
    )
    out_specs = P("seq", "head")
    return jax.shard_map(
        on_device, mesh=mesh, in_specs=in_specs, out_specs=out_specs, check_vma=False
    )
```
